32 devices in a mesh: chan: 8 (over y, x, core), day: 4 (over z).
Axes of the slice: x: 2, y: 2, z: 4, core: 2. Of those that a mesh axis runs over, the one named last changes fastest.
Arguments:
- records: bfloat16 [4, 512, 4096], P('day', 'chan'), may hold values from -50 to 50
- filter_taps: bfloat16 [64], replicated, may hold values from -0.75 to 0.75
- window_offsets: int32 [4, 2], P('day'), may hold values from 0 to 3009, as said below
- pair_masks: int32 [3], replicated, may hold values from 1 to 7, as said below
Outputs:
- stacks: float32 [3, 65, 32768], P(None, None, ('chan', 'day'))
The draws below stay inside these ranges and needn't reach their ends.
Inputs may be any that keep to these rules, and one draw needn't show every extreme that they name: `window_offsets`: in each day group one window ends at the record's last sample. `pair_masks`: the masks are distinct; 1 and 7 are among them.
All inputs are finite; a program needn't handle non-finite values.
Results may differ from the reference program's by a relative error of at most 0.0029.
Values may be sent and summed in bfloat16 or wider, within the bound.
No kernel may reach another device: no remote copies, remote signals or barrier semaphores. Data moves between devices by JAX's collectives and lax.ppermute only.
A program may use at most 64 MiB of HBM per device.

```python
import jax
import jax.numpy as jnp
from jax import lax

C_BLK = 64
L = 1024
TAPS = 64
MAXLAG = 32
ROUNDS = 3
WIN = 2
LAGS = 65
REC = 4096
MAXOFF = 3009
CHANNELS = 512
DAYS = 4


def draw_records(key, part):
    first_key, second_key = jax.random.split(jax.random.fold_in(key, 11))
    shape = (DAYS, CHANNELS, REC)
    base = jnp.clip(jax.random.normal(first_key, shape, jnp.float32), -5.0, 5.0)
    spread = jnp.log(10.0)
    scales = jnp.exp(jax.random.uniform(second_key, (DAYS, CHANNELS, 1), jnp.float32) * spread)
    return (base * scales).astype(jnp.bfloat16)


def draw_window_offsets(key, part):
    first_key, second_key = jax.random.split(jax.random.fold_in(key, 23))
    values = jax.random.randint(first_key, (DAYS, WIN), 0, MAXOFF + 1, jnp.int32)
    places = jax.random.randint(second_key, (DAYS, 1), 0, WIN, jnp.int32)
    columns = jnp.arange(WIN, dtype=jnp.int32)[None, :]
    values = jnp.where(columns == places, MAXOFF, values)
    return values.astype(jnp.int32)


def draw_pair_masks(key, part):
    first_key, second_key = jax.random.split(jax.random.fold_in(key, 37))
    blocks_count = CHANNELS // C_BLK
    middle = jax.random.permutation(first_key, jnp.arange(2, blocks_count - 1, dtype=jnp.int32))[:ROUNDS - 2]
    chosen = jnp.concatenate([jnp.array([1, blocks_count - 1], jnp.int32), middle])
    return jax.random.permutation(second_key, chosen).astype(jnp.int32)


def scatter_about(own_key, shape, deviation, limit, kind=jnp.bfloat16):
    return jnp.clip(deviation * jax.random.normal(own_key, shape, jnp.float32), -limit, limit).astype(kind)


def setup_inputs(seed: int = 0) -> dict:
    keys = jax.random.split(jax.random.key(seed), 5)
    return {
        "records": draw_records(jax.random.fold_in(keys[4], 71), 0),
        "filter_taps": scatter_about(keys[1], (TAPS,), TAPS ** -0.5, 0.75),
        "window_offsets": draw_window_offsets(jax.random.fold_in(keys[4], 71), 0),
        "pair_masks": draw_pair_masks(jax.random.fold_in(keys[4], 71), 0),
    }


def whiten(segments, filter_taps):
    tap_count = filter_taps.shape[0]
    width = segments.shape[-1] - tap_count + 1
    taps_wide = filter_taps.astype(jnp.float32)
    total = jnp.zeros(segments.shape[:-1] + (width,), jnp.float32)
    for tap_index in range(tap_count):
        total = total + taps_wide[tap_index] * segments[..., tap_index:tap_index + width].astype(jnp.float32)
    power = lax.optimization_barrier(jnp.mean(total * total, axis=-1, keepdims=True))
    return (total * lax.rsqrt(power + 1e-06)).astype(jnp.bfloat16)

def reference(records, filter_taps, window_offsets, pair_masks):
    seg_len = L + TAPS - 1
    blocks_count = CHANNELS // C_BLK

    def cut_day(record, offsets_day):

        def cut_window(start):
            return lax.dynamic_slice(record, (jnp.zeros((), jnp.int32), start.astype(jnp.int32)), (CHANNELS, seg_len))
        return jax.vmap(cut_window)(offsets_day)
    segments = jax.vmap(cut_day)(records, window_offsets)
    white = whiten(segments, filter_taps)
    blocks = jnp.transpose(white, (2, 0, 1, 3)).reshape(blocks_count, C_BLK, DAYS, WIN, L)
    padded = jnp.pad(blocks, ((0, 0), (0, 0), (0, 0), (0, 0), (MAXLAG, MAXLAG)))
    results = []
    for round_index in range(ROUNDS):
        mask_value = pair_masks[round_index]

        def one_block(block_index):
            mine = blocks[block_index].astype(jnp.float32)
            theirs = padded[jnp.bitwise_xor(block_index, mask_value)].astype(jnp.float32)

            def one_lag(lag_index):
                shifted = lax.dynamic_slice_in_dim(theirs, lag_index, L, axis=3)
                return jnp.einsum('cxwt,dxwt->cd', mine, shifted, precision=lax.Precision.HIGHEST)
            return lax.map(one_lag, jnp.arange(LAGS, dtype=jnp.int32))
        tables = lax.map(one_block, jnp.arange(blocks_count, dtype=jnp.int32))
        tables = jnp.transpose(tables, (1, 0, 2, 3)).reshape(LAGS, CHANNELS * C_BLK)
        results.append(tables)
    norm_factor = 1.0 / jnp.sqrt(jnp.float32(DAYS * WIN * L))
    return jnp.stack(results) * norm_factor
```

```python
import functools

import jax
import jax.numpy as jnp
from jax import lax
from jax.experimental import pallas as pl
from jax.experimental.pallas import tpu as pltpu
from jax.sharding import PartitionSpec as P

L = 1024
MAXLAG = 32
LAGS = 2 * MAXLAG + 1
FINE = 16
COARSE = 4
PAD = 1152
CUT = 1280
NT = (((1,), (1,)), ((), ()))


def vmem(shape=None):
    return pl.BlockSpec(memory_space=pltpu.VMEM)


def smem():
    return pl.BlockSpec(memory_space=pltpu.SMEM)


def whiten_kernel(off_ref, taps_ref, rec_ref, out_ref, wide_ref):
    chans, rec_len = rec_ref.shape[1], rec_ref.shape[2]
    taps = taps_ref[...].astype(jnp.float32)
    row = jnp.concatenate([taps, jnp.zeros((1, 384 - taps.shape[1]), jnp.float32)], axis=1)
    row = jnp.broadcast_to(row, (8, 384))
    bands = []
    wide_ref[...] = jnp.zeros_like(wide_ref)
    for w in range(2):
        start = off_ref[0, w]
        base = jnp.minimum((start // 128) * 128, rec_len - CUT)
        base = pl.multiple_of(base, 128)
        moved = pltpu.roll(row, start - base, 1)
        block = jnp.broadcast_to(moved[0:1], (128, 384))
        block = pltpu.roll(block, 0, 1, stride=1, stride_axis=0).astype(jnp.bfloat16)
        none = jnp.zeros((128, 128), jnp.bfloat16)
        bands.append(
            jnp.concatenate(
                [jnp.concatenate([block, none], axis=1), jnp.concatenate([none, block], axis=1)],
                axis=0,
            )
        )
        wide_ref[w, w * chans : (w + 1) * chans, :] = rec_ref[0, :, pl.ds(base, CUT)]
    parts = []
    for c in range(L // 256):
        part = lax.dot_general(
            bands[0], wide_ref[0, :, c * 256 : c * 256 + 512], NT, preferred_element_type=jnp.float32
        )
        part += lax.dot_general(
            bands[1], wide_ref[1, :, c * 256 : c * 256 + 512], NT, preferred_element_type=jnp.float32
        )
        parts.append(part)
    power = sum(jnp.sum(part * part, axis=0, keepdims=True) for part in parts) * (1.0 / L)
    scale = lax.rsqrt(power + 1e-06)
    for c, part in enumerate(parts):
        out_ref[c * 256 : (c + 1) * 256, :] = (part * scale).astype(jnp.bfloat16)


def prepare_kernel(days, white_ref, keep_ref, send_ref):
    chans = white_ref.shape[1] // 2
    share = chans // days
    bits = days.bit_length() - 1
    me = lax.axis_index("day")
    rows = lax.broadcasted_iota(jnp.int32, (2 * chans, 2 * chans), 0)
    cols = lax.broadcasted_iota(jnp.int32, (2 * chans, 2 * chans), 1)
    place = (rows % chans) // share
    slot = jnp.zeros_like(place)
    for b in range(bits):
        slot = slot + (((place >> b) & 1) << (bits - 1 - b))
    source = (rows // chans) * chans + (slot ^ me) * share + rows % share
    pick = (cols == source).astype(jnp.float32).astype(jnp.bfloat16)
    mine = lax.dot_general(pick, white_ref[...], NT, preferred_element_type=jnp.float32)
    mine = jnp.concatenate([mine, jnp.zeros((2 * chans, PAD - L), jnp.float32)], axis=1)
    half = chans // 2
    for p in range(FINE + 1):
        moved = (pltpu.roll(mine, p, 1) if p else mine).astype(jnp.bfloat16)
        for w in range(2):
            span = slice(w * PAD, (w + 1) * PAD)
            keep_ref[p * half : (p + 1) * half, span] = moved[w * chans : w * chans + half]
            send_ref[p * half : (p + 1) * half, span] = moved[w * chans + half : (w + 1) * chans]


def correlate_kernel(theirs_ref, keep_ref, send_ref, kept_ref, sent_ref, w_ref):
    theirs = theirs_ref[...].astype(jnp.float32)
    swapped = pltpu.roll(theirs, 64, 1)
    low = lax.broadcasted_iota(jnp.int32, (1, 128), 1) < 64
    zero = jnp.zeros((16, 128), jnp.float32)
    for w, (a, b) in enumerate(((theirs, swapped), (swapped, theirs))):
        first = jnp.concatenate([zero, zero, a, zero, zero, zero, zero], axis=0)
        second = jnp.concatenate([zero, b, zero, zero, zero, zero, zero], axis=0)
        both = jnp.where(low, first, second).astype(jnp.bfloat16)
        rows = both.shape[0]
        w_ref[w * PAD : w * PAD + rows, 0:128] = both
        w_ref[w * PAD + rows : (w + 1) * PAD, 0:128] = jnp.zeros((PAD - rows, 128), jnp.bfloat16)
        w_ref[w * PAD : w * PAD + rows - 32, 128:256] = both[32:]
        w_ref[w * PAD + rows - 32 : (w + 1) * PAD, 128:256] = jnp.zeros((PAD - rows + 32, 128), jnp.bfloat16)
    weights = w_ref[...]
    sent_ref[...] = jnp.dot(send_ref[...], weights, preferred_element_type=jnp.float32).astype(jnp.bfloat16)
    kept_ref[...] = jnp.dot(keep_ref[...], weights, preferred_element_type=jnp.float32)


def finish_kernel(share, norm, order_ref, *refs):
    ins, out_ref, s_ref = refs[:-2], refs[-2], refs[-1]
    low = lax.broadcasted_iota(jnp.int32, (1, 128), 1) < 64
    for k in range(len(ins) // 2):
        total = (ins[2 * k][...] + ins[2 * k + 1][...].astype(jnp.float32)) * norm
        s_ref[0] = total[:, 0:128]
        s_ref[1] = total[:, 128:256]
        r = order_ref[k]
        for pair in range(share // 2):
            for tile in range(COARSE // 2):
                one = s_ref[tile, pl.ds(2 * pair, FINE, stride=share), :]
                two = s_ref[tile, pl.ds(2 * pair + 1, FINE, stride=share), :]
                to = slice(pair * 128, pair * 128 + 128)
                q = 2 * tile * FINE
                out_ref[r, q : q + FINE, to] = jnp.where(low, one, pltpu.roll(two, 64, 1))
                out_ref[r, q + FINE : q + 2 * FINE, to] = jnp.where(low, pltpu.roll(one, 64, 1), two)
            one = s_ref[1, FINE * share + 2 * pair : FINE * share + 2 * pair + 1, :]
            two = s_ref[1, FINE * share + 2 * pair + 1 : FINE * share + 2 * pair + 2, :]
            out_ref[r, LAGS - 1 : LAGS, pair * 128 : pair * 128 + 128] = jnp.where(low, pltpu.roll(one, 64, 1), two)


def apart(value, axis, mask):
    return lax.ppermute(value, axis, [(s, s ^ mask) for s in range(lax.axis_size(axis))])


def local(records, filter_taps, window_offsets, pair_masks):
    chans = records.shape[1]
    blocks = lax.axis_size("chan")
    days = lax.axis_size("day")
    share = chans // days
    params = pltpu.CompilerParams(vmem_limit_bytes=40 * 1024 * 1024)
    white = pl.pallas_call(
        whiten_kernel,
        out_shape=jax.ShapeDtypeStruct((L, 2 * chans), jnp.bfloat16),
        in_specs=[smem(), vmem(), vmem()],
        out_specs=vmem(),
        scratch_shapes=[pltpu.VMEM((2, 2 * chans, CUT), jnp.bfloat16)],
        compiler_params=params,
    )(window_offsets, filter_taps.reshape(1, -1), records)

    last = blocks - 1
    third = pair_masks[0] ^ pair_masks[1] ^ pair_masks[2] ^ 1 ^ last
    near = apart(white, "chan", 1)
    if blocks == 8:
        along_x = apart(white, "chan", 2)
        along_y = apart(white, "chan", 4)
        far = apart(white, "chan", last)
        chip = third >> 1
        held = jnp.where(chip == 3, far, jnp.where(chip == 1, along_x, along_y))
        other = apart(held, "chan", 1)
        free = jnp.where((third == 2) | (third == 4), held, other)
    else:
        far = apart(white, "chan", last)
        free = white
        for bit in range(blocks.bit_length() - 1):
            free = jnp.where(((third >> bit) & 1) == 1, apart(free, "chan", 2**bit), free)
    order = jnp.stack([jnp.argmax(pair_masks == m).astype(jnp.int32) for m in (jnp.int32(1), jnp.int32(last), third)])

    half_rows = (FINE + 1) * chans // 2
    keep, send = pl.pallas_call(
        functools.partial(prepare_kernel, days),
        out_shape=[jax.ShapeDtypeStruct((half_rows, 2 * PAD), jnp.bfloat16)] * 2,
        in_specs=[vmem()],
        out_specs=[vmem()] * 2,
        compiler_params=params,
    )(white)

    def correlate(theirs):
        kept, sent = pl.pallas_call(
            correlate_kernel,
            out_shape=[
                jax.ShapeDtypeStruct((half_rows, 256), jnp.float32),
                jax.ShapeDtypeStruct((half_rows, 256), jnp.bfloat16),
            ],
            in_specs=[vmem()] * 3,
            out_specs=[vmem()] * 2,
            scratch_shapes=[pltpu.VMEM((2 * PAD, 256), jnp.bfloat16)],
            compiler_params=params,
        )(theirs, keep, send)
        shape = (FINE + 1, chans // 2, 256)
        return kept.reshape(shape), sent.reshape(shape)

    finals = []
    for theirs in (near, far, free):
        kept, sent = correlate(theirs)
        step = 1
        while step < days:
            came = apart(sent, "day", step)
            step *= 2
            if step < days:
                total = kept + came.astype(jnp.float32)
                half = total.shape[1] // 2
                kept = total[:, :half]
                sent = total[:, half:].astype(jnp.bfloat16)
        rows = (FINE + 1) * share
        finals += [kept.reshape(rows, 256), came.reshape(rows, 256)]

    day_total = records.shape[0] * days
    norm = float((day_total * window_offsets.shape[1] * L) ** -0.5)
    return pl.pallas_call(
        functools.partial(finish_kernel, share, norm),
        out_shape=jax.ShapeDtypeStruct((3, LAGS, share * chans), jnp.float32),
        in_specs=[smem()] + [vmem()] * 6,
        out_specs=vmem(),
        scratch_shapes=[pltpu.VMEM((2, (FINE + 1) * share, 128), jnp.float32)],
        compiler_params=params,
    )(order, *finals)


def solution(mesh):
    in_specs = (P("day", "chan", None), P(), P("day", None), P())
    out_specs = P(None, None, ("chan", "day"))
    return jax.shard_map(local, mesh=mesh, in_specs=in_specs, out_specs=out_specs, check_vma=False)
```

```python
import functools

import jax
import jax.numpy as jnp
from jax import lax
from jax.experimental import pallas as pl
from jax.experimental.pallas import tpu as pltpu
from jax.sharding import PartitionSpec as P

L = 1024
MAXLAG = 32
LAGS = 2 * MAXLAG + 1
FINE = 16
COARSE = 4
PLANES = FINE + 1
PAD = 1152
CUT = 1280
COST = 1.0
DIRECT_ORDER = (2, 3, 1)
FAR_AFTER = False
LAST_AFTER = 1
LATE_Z = False
NEAR_FIRST = False
FAR, FREE = "low", "low"
NT = (((1,), (1,)), ((), ()))
VMEM = pl.BlockSpec(memory_space=pltpu.VMEM)
SMEM = pl.BlockSpec(memory_space=pltpu.SMEM)
HBM = pl.BlockSpec(memory_space=pltpu.HBM)


def call(kernel, out_shape, in_specs, scratch=(), micros=1.0, vmem=24):
    many = isinstance(out_shape, list)
    return pl.pallas_call(
        kernel,
        out_shape=out_shape,
        in_specs=in_specs,
        out_specs=[VMEM] * len(out_shape) if many else VMEM,
        scratch_shapes=list(scratch),
        compiler_params=pltpu.CompilerParams(vmem_limit_bytes=vmem * 1024 * 1024),
        cost_estimate=pl.CostEstimate(flops=int(micros * COST * 1e9), bytes_accessed=int(micros * COST * 3e6), transcendentals=0),
    )


def whiten_kernel(off_hbm, taps_hbm, rec_hbm, out_ref, off_ref, taps_ref, rec_ref, wide_ref, sems):
    copies = [
        pltpu.make_async_copy(src, dst, sems.at[k])
        for k, (src, dst) in enumerate(((off_hbm, off_ref), (rec_hbm, rec_ref), (taps_hbm, taps_ref)))
    ]
    for copy in copies:
        copy.start()
    chans, rec_len = rec_ref.shape[1], rec_ref.shape[2]
    wide_ref[...] = jnp.zeros_like(wide_ref)
    copies[2].wait()
    copies[0].wait()
    taps = taps_ref[...].astype(jnp.float32)
    row = jnp.concatenate([taps, jnp.zeros((1, 384 - taps.shape[1]), jnp.float32)], axis=1)
    row = jnp.broadcast_to(row, (8, 384))
    bands, bases = [], []
    for w in range(2):
        start = off_ref[0, w]
        base = jnp.minimum((start // 128) * 128, rec_len - CUT)
        bases.append(pl.multiple_of(base, 128))
        moved = pltpu.roll(row, start - base, 1)
        block = jnp.broadcast_to(moved[0:1], (128, 384))
        block = pltpu.roll(block, 0, 1, stride=1, stride_axis=0).astype(jnp.bfloat16)
        none = jnp.zeros((128, 128), jnp.bfloat16)
        bands.append(
            jnp.concatenate(
                [jnp.concatenate([block, none], axis=1), jnp.concatenate([none, block], axis=1)],
                axis=0,
            )
        )
    copies[1].wait()
    for w in range(2):
        wide_ref[w, w * chans : (w + 1) * chans, :] = rec_ref[0, :, pl.ds(bases[w], CUT)]
    parts = []
    for c in range(L // 256):
        part = lax.dot_general(
            bands[0], wide_ref[0, :, c * 256 : c * 256 + 512], NT, preferred_element_type=jnp.float32
        )
        part += lax.dot_general(
            bands[1], wide_ref[1, :, c * 256 : c * 256 + 512], NT, preferred_element_type=jnp.float32
        )
        parts.append(part)
    power = sum(jnp.sum(part * part, axis=0, keepdims=True) for part in parts) * (1.0 / L)
    scale = lax.rsqrt(power + 1e-06)
    for c, part in enumerate(parts):
        out_ref[c * 256 : (c + 1) * 256, :] = (part * scale).astype(jnp.bfloat16)


def prepare_kernel(days, count, white_ref, lhs_ref):
    chans = white_ref.shape[1] // 2
    share = chans // days
    bits = days.bit_length() - 1
    me = lax.axis_index("day")
    rows = lax.broadcasted_iota(jnp.int32, (2 * chans, 2 * chans), 0)
    cols = lax.broadcasted_iota(jnp.int32, (2 * chans, 2 * chans), 1)
    place = (rows % chans) // share
    slot = jnp.zeros_like(place)
    for b in range(bits):
        slot = slot + (((place >> b) & 1) << (bits - 1 - b))
    source = (rows // chans) * chans + (slot ^ me) * share + rows % share
    pick = (cols == source).astype(jnp.float32).astype(jnp.bfloat16)
    mine = lax.dot_general(pick, white_ref[...], NT, preferred_element_type=jnp.float32)
    mine = jnp.concatenate([mine, jnp.zeros((2 * chans, PAD - L), jnp.float32)], axis=1)
    for p in range(PLANES):
        moved = (pltpu.roll(mine, p, 1) if p else mine).astype(jnp.bfloat16)
        for w in range(2):
            for b in range(count):
                at = (b * PLANES + p) * share
                lhs_ref[at : at + share, w * PAD : (w + 1) * PAD] = moved[w * chans + b * share : w * chans + (b + 1) * share]


def fill_weights(theirs, w_ref):
    theirs = theirs.astype(jnp.float32)
    swapped = pltpu.roll(theirs, 64, 1)
    low = lax.broadcasted_iota(jnp.int32, (1, 128), 1) < 64
    zero = jnp.zeros((16, 128), jnp.float32)
    for w, (a, b) in enumerate(((theirs, swapped), (swapped, theirs))):
        first = jnp.concatenate([zero, zero, a, zero, zero, zero, zero], axis=0)
        second = jnp.concatenate([zero, b, zero, zero, zero, zero, zero], axis=0)
        both = jnp.where(low, first, second).astype(jnp.bfloat16)
        rows = both.shape[0]
        w_ref[w * PAD : w * PAD + rows, 0:128] = both
        w_ref[w * PAD + rows : (w + 1) * PAD, 0:128] = jnp.zeros((PAD - rows, 128), jnp.bfloat16)
        w_ref[w * PAD : w * PAD + rows - 32, 128:256] = both[32:]
        w_ref[w * PAD + rows - 32 : (w + 1) * PAD, 128:256] = jnp.zeros((PAD - rows + 32, 128), jnp.bfloat16)


def correlate(places, theirs, lhs_ref, out_refs, w_ref):
    fill_weights(theirs, w_ref)
    weights = w_ref[...]
    half = lhs_ref.shape[0] // 2
    size = lhs_ref.shape[0] // len(places)
    for base in (half, 0):
        part = jnp.dot(lhs_ref[base : base + half, :], weights, preferred_element_type=jnp.float32)
        for place, (index, at) in enumerate(places):
            row = place * size - base
            if 0 <= row < half:
                ref = out_refs[index]
                ref[at * size : (at + 1) * size, :] = part[row : row + size].astype(ref.dtype)


def paired_kernel(theirs_ref, lhs_ref, theirs2_ref, lhs2_ref, kept_ref, sent_ref, w_ref, sum_ref):
    half = lhs2_ref.shape[0]
    fill_weights(theirs_ref[...], w_ref)
    sum_ref[...] = jnp.dot(lhs_ref[0:half, :], w_ref[...], preferred_element_type=jnp.float32)
    fill_weights(theirs2_ref[...], w_ref)
    total = sum_ref[...] + jnp.dot(lhs2_ref[...], w_ref[...], preferred_element_type=jnp.float32)
    size = kept_ref.shape[0]
    kept_ref[...] = total[0:size]
    sent_ref[...] = total[size:].astype(jnp.bfloat16)


def known_kernel(places, theirs_ref, lhs_ref, *refs):
    correlate(places, theirs_ref[...], lhs_ref, refs[:-1], refs[-1])


def third_mask(masks_ref, last):
    return masks_ref[0] ^ masks_ref[1] ^ masks_ref[2] ^ 1 ^ last


def other_core(third):
    return (third == 3) | (third == 5)


def passed_kernel(last, masks_ref, white_ref, near_ref, out_ref):
    flip = other_core(third_mask(masks_ref, last))

    @pl.when(flip)
    def _():
        out_ref[...] = near_ref[...]

    @pl.when(jnp.logical_not(flip))
    def _():
        out_ref[...] = white_ref[...]


def chosen_kernel(places, last, masks_ref, x_ref, y_ref, corner_ref, lhs_ref, *refs):
    outs, w_ref, theirs_ref = refs[:-2], refs[-2], refs[-1]
    chip = third_mask(masks_ref, last) >> 1
    for k, ref in enumerate((x_ref, y_ref, corner_ref)):

        @pl.when(chip == k + 1)
        def _(ref=ref):
            theirs_ref[...] = ref[...]

    correlate(places, theirs_ref[...], lhs_ref, outs, w_ref)


def finish_kernel(share, norm, last, counts, masks_ref, *refs):
    ins, out_ref, s_ref = list(refs[:-2]), refs[-2], refs[-1]
    low = lax.broadcasted_iota(jnp.int32, (1, 128), 1) < 64
    third = third_mask(masks_ref, last)
    rows = PLANES * share
    for k, mask in enumerate((1, last, third)):
        total = sum(ins.pop(0)[0:rows, :].astype(jnp.float32) for _ in range(counts[k])) * norm
        s_ref[0] = total[:, 0:128]
        s_ref[1] = total[:, 128:256]
        r = jnp.where(masks_ref[0] == mask, 0, jnp.where(masks_ref[1] == mask, 1, 2))
        for pair in range(share // 2):
            to = slice(pair * 128, pair * 128 + 128)
            for tile in range(COARSE // 2):
                one = s_ref[tile, pl.ds(2 * pair, FINE, stride=share), :]
                two = s_ref[tile, pl.ds(2 * pair + 1, FINE, stride=share), :]
                q = 2 * tile * FINE
                out_ref[r, q : q + FINE, to] = jnp.where(low, one, pltpu.roll(two, 64, 1))
                out_ref[r, q + FINE : q + 2 * FINE, to] = jnp.where(low, pltpu.roll(one, 64, 1), two)
            one = s_ref[1, FINE * share + 2 * pair : FINE * share + 2 * pair + 1, :]
            two = s_ref[1, FINE * share + 2 * pair + 1 : FINE * share + 2 * pair + 2, :]
            out_ref[r, LAGS - 1 : LAGS, to] = jnp.where(low, pltpu.roll(one, 64, 1), two)


def apart(value, axis, mask):
    return lax.ppermute(value, axis, [(s, s ^ mask) for s in range(lax.axis_size(axis))])


def local(records, filter_taps, window_offsets, pair_masks):
    chans, rec_len = records.shape[1], records.shape[2]
    taps = filter_taps.shape[0]
    blocks = lax.axis_size("chan")
    days = lax.axis_size("day")
    share = chans // days
    last = blocks - 1
    bf16, f32 = jnp.bfloat16, jnp.float32
    white = call(
        whiten_kernel,
        jax.ShapeDtypeStruct((L, 2 * chans), bf16),
        [HBM] * 3,
        [
            pltpu.SMEM((1, 2), jnp.int32),
            pltpu.VMEM((1, taps), bf16),
            pltpu.VMEM((1, chans, rec_len), bf16),
            pltpu.VMEM((2, 2 * chans, CUT), bf16),
            pltpu.SemaphoreType.DMA((3,)),
        ],
        micros=2.0,
        vmem=63,
    )(window_offsets, filter_taps.reshape(1, -1), records)

    near = apart(white, "chan", 1)
    far = apart(white, "chan", last)
    if days == 4:
        white2 = apart(lax.optimization_barrier((white, near))[0] if LATE_Z else white, "day", 1)

    def prepare(block, count):
        return call(
            functools.partial(prepare_kernel, days, count),
            jax.ShapeDtypeStruct((PLANES * share * count, 2 * PAD), bf16),
            [VMEM],
            micros=1.5,
        )(block)

    lhs = prepare(white, days)

    slot_rows = PLANES * share
    weights = pltpu.VMEM((2 * PAD, 256), bf16)

    def reverse(slot):
        return sum(((slot >> b) & 1) << (days.bit_length() - 2 - b) for b in range(days.bit_length() - 1))

    def plan(mode):
        if mode == "direct":
            return list(DIRECT_ORDER), [([slot], bf16 if slot else f32) for slot in range(days)]
        steps = [1 << b for b in range(days.bit_length() - 1)]
        if mode == "high":
            steps = steps[::-1]
        left, outs = list(range(days)), []
        for step in steps:
            outs.insert(0, ([slot for slot in left if slot & step], bf16 if len(left) == days else f32))
            left = [slot for slot in left if not slot & step]
        return steps, [(left, f32)] + outs

    def started(mode, steps, outs, parts):
        if mode == "direct":
            came = [parts[0]] + [apart(parts[s], "day", s) for s in steps]
            return lambda after=None: came
        kept = list(parts[:-1])
        came = [apart(parts[-1], "day", steps[0])]
        held = [[slot ^ steps[0] for slot in outs[-1][0]]]

        def rest(after=None):
            if after is not None:
                came[0], _ = lax.optimization_barrier((came[0], after))
            for step in steps[1:]:
                piece, slots = kept.pop(), outs[len(kept)][0]
                n = piece.shape[0]
                for c, slots_c in zip(came, held):
                    at = slots_c.index(slots[0]) * slot_rows
                    piece = piece + c[at : at + n].astype(f32)
                held.append([slot ^ step for slot in slots])
                came.append(apart(piece.astype(bf16), "day", step))
            return [kept[0]] + came

        rest.came = came
        return rest

    def day_sum(mode, theirs, pick=None):
        mode = mode if days == 4 else "low"
        steps, outs = plan(mode)
        shapes = [jax.ShapeDtypeStruct((len(slots) * slot_rows, 256), kind) for slots, kind in outs]
        where = {slot: (k, at) for k, (slots, _) in enumerate(outs) for at, slot in enumerate(slots)}
        places = [where[reverse(place)] for place in range(days)]
        if pick is None:
            parts = call(functools.partial(known_kernel, places), shapes, [VMEM] * 2, [weights], micros=2.0)(theirs, lhs)
        else:
            parts = call(
                functools.partial(chosen_kernel, places, last),
                shapes,
                [SMEM] + [VMEM] * (len(theirs) + 1),
                [weights, pltpu.VMEM((L, 2 * chans), bf16)],
                micros=2.0,
            )(pick, *theirs, lhs)
        return parts[-1], started(mode, steps, outs, parts)

    if blocks == 8:
        passed = call(
            functools.partial(passed_kernel, last),
            jax.ShapeDtypeStruct(white.shape, bf16),
            [SMEM] + [VMEM] * 2,
            micros=0.5,
        )(pair_masks, white, near)
        along_x = apart(passed, "chan", 2)
        along_y = apart(passed, "chan", 4)
    far_done, far_sum = day_sum(FAR, far)
    if days == 4:
        white2, _ = lax.optimization_barrier((white2, far_done))
        near2 = apart(white2, "chan", 1)
        near_kept, near_done = call(
            paired_kernel,
            [jax.ShapeDtypeStruct((slot_rows, 256), f32), jax.ShapeDtypeStruct((slot_rows, 256), bf16)],
            [VMEM] * 4,
            [weights, pltpu.VMEM((2 * slot_rows, 256), f32)],
            micros=2.0,
        )(near, lhs, near2, prepare(white2, 2))
        near_came = [near_kept, apart(near_done, "day", 2)]
    else:
        near_done, near_sum = day_sum("low", near)
        near_came = near_sum()
    if blocks == 8:
        corner = apart(far, "chan", 1)
        if NEAR_FIRST:
            along_x, along_y, _ = lax.optimization_barrier((along_x, along_y, near_done))
        free_done, free_sum = day_sum(FREE, (along_x, along_y, corner), pair_masks)
    else:
        free = white
        third = pair_masks[0] ^ pair_masks[1] ^ pair_masks[2] ^ 1 ^ last
        for bit in range(blocks.bit_length() - 1):
            free = jnp.where(((third >> bit) & 1) == 1, apart(free, "chan", 2**bit), free)
        free_done, free_sum = day_sum(FREE, free)
    far_came = far_sum(free_done if FAR_AFTER else None)
    sums = [near_came, far_came, free_sum((None, near_came[-1], (near_came[-1], far_came[-1]))[LAST_AFTER])]

    day_total = records.shape[0] * days
    norm = float((day_total * window_offsets.shape[1] * L) ** -0.5)
    flat = [part for group in sums for part in group]
    return call(
        functools.partial(finish_kernel, share, norm, last, [len(group) for group in sums]),
        jax.ShapeDtypeStruct((3, LAGS, share * chans), f32),
        [SMEM] + [VMEM] * len(flat),
        [pltpu.VMEM((2, slot_rows, 128), f32)],
        micros=2.0,
    )(pair_masks, *flat)


def solution(mesh):
    in_specs = (P("day", "chan", None), P(), P("day", None), P())
    out_specs = P(None, None, ("chan", "day"))
    return jax.shard_map(local, mesh=mesh, in_specs=in_specs, out_specs=out_specs, check_vma=False)
```

```python
import functools

import jax
import jax.numpy as jnp
from jax import lax
from jax.experimental import pallas as pl
from jax.experimental.pallas import tpu as pltpu
from jax.sharding import PartitionSpec as P

L = 1024
MAXLAG = 32
LAGS = 2 * MAXLAG + 1
FINE = 16
COARSE = 4
PLANES = FINE + 1
PAD = 1152
CUT = 1280
COST = 1.0
DIRECT_ORDER = (2, 3, 1)
FAR_AFTER = False
LAST_AFTER = 1
LATE_Z = False
FAR_FIRST = True
EARLY = False
NEAR_FIRST = False
FAR, FREE = "low", "low"
NT = (((1,), (1,)), ((), ()))
VMEM = pl.BlockSpec(memory_space=pltpu.VMEM)
SMEM = pl.BlockSpec(memory_space=pltpu.SMEM)
HBM = pl.BlockSpec(memory_space=pltpu.HBM)


def call(kernel, out_shape, in_specs, scratch=(), micros=1.0, vmem=24):
    many = isinstance(out_shape, list)
    return pl.pallas_call(
        kernel,
        out_shape=out_shape,
        in_specs=in_specs,
        out_specs=[VMEM] * len(out_shape) if many else VMEM,
        scratch_shapes=list(scratch),
        compiler_params=pltpu.CompilerParams(vmem_limit_bytes=vmem * 1024 * 1024),
        cost_estimate=pl.CostEstimate(flops=int(micros * COST * 1e9), bytes_accessed=int(micros * COST * 3e6), transcendentals=0),
    )


def whiten_kernel(off_hbm, taps_hbm, rec_hbm, out_ref, off_ref, taps_ref, rec_ref, wide_ref, sems):
    copies = [
        pltpu.make_async_copy(src, dst, sems.at[k])
        for k, (src, dst) in enumerate(((off_hbm, off_ref), (rec_hbm, rec_ref), (taps_hbm, taps_ref)))
    ]
    for copy in copies:
        copy.start()
    chans, rec_len = rec_ref.shape[1], rec_ref.shape[2]
    wide_ref[...] = jnp.zeros_like(wide_ref)
    copies[2].wait()
    copies[0].wait()
    taps = taps_ref[...].astype(jnp.float32)
    row = jnp.concatenate([taps, jnp.zeros((1, 384 - taps.shape[1]), jnp.float32)], axis=1)
    row = jnp.broadcast_to(row, (8, 384))
    bands, bases = [], []
    for w in range(2):
        start = off_ref[0, w]
        base = jnp.minimum((start // 128) * 128, rec_len - CUT)
        bases.append(pl.multiple_of(base, 128))
        moved = pltpu.roll(row, start - base, 1)
        block = jnp.broadcast_to(moved[0:1], (128, 384))
        block = pltpu.roll(block, 0, 1, stride=1, stride_axis=0).astype(jnp.bfloat16)
        none = jnp.zeros((128, 128), jnp.bfloat16)
        bands.append(
            jnp.concatenate(
                [jnp.concatenate([block, none], axis=1), jnp.concatenate([none, block], axis=1)],
                axis=0,
            )
        )
    copies[1].wait()
    for w in range(2):
        wide_ref[w, w * chans : (w + 1) * chans, :] = rec_ref[0, :, pl.ds(bases[w], CUT)]
    parts = []
    for c in range(0, L, 512):
        pair = 0.0
        for w in range(2):
            both = jnp.concatenate([wide_ref[w, :, c : c + 512], wide_ref[w, :, c + 256 : c + 768]], axis=0)
            pair += lax.dot_general(bands[w], both, NT, preferred_element_type=jnp.float32)
        parts += [pair[:, 0:128], pair[:, 128:256]]
    power = sum(jnp.sum(part * part, axis=0, keepdims=True) for part in parts) * (1.0 / L)
    scale = lax.rsqrt(power + 1e-06)
    for c, part in enumerate(parts):
        out_ref[c * 256 : (c + 1) * 256, :] = (part * scale).astype(jnp.bfloat16)


def prepare_kernel(days, count, white_ref, lhs_ref):
    chans = white_ref.shape[1] // 2
    share = chans // days
    bits = days.bit_length() - 1
    me = lax.axis_index("day")
    rows = lax.broadcasted_iota(jnp.int32, (2 * chans, 2 * chans), 0)
    cols = lax.broadcasted_iota(jnp.int32, (2 * chans, 2 * chans), 1)
    place = (rows % chans) // share
    slot = jnp.zeros_like(place)
    for b in range(bits):
        slot = slot + (((place >> b) & 1) << (bits - 1 - b))
    source = (rows // chans) * chans + (slot ^ me) * share + rows % share
    pick = (cols == source).astype(jnp.float32).astype(jnp.bfloat16)
    mine = lax.dot_general(pick, white_ref[...], NT, preferred_element_type=jnp.float32)
    mine = jnp.concatenate([mine, jnp.zeros((2 * chans, PAD - L), jnp.float32)], axis=1)
    for p in range(PLANES):
        moved = (pltpu.roll(mine, p, 1) if p else mine).astype(jnp.bfloat16)
        for w in range(2):
            for b in range(count):
                at = (b * PLANES + p) * share
                lhs_ref[at : at + share, w * PAD : (w + 1) * PAD] = moved[w * chans + b * share : w * chans + (b + 1) * share]


def fill_weights(theirs, w_ref):
    theirs = theirs.astype(jnp.float32)
    swapped = pltpu.roll(theirs, 64, 1)
    low = lax.broadcasted_iota(jnp.int32, (1, 128), 1) < 64
    zero = jnp.zeros((16, 128), jnp.float32)
    for w, (a, b) in enumerate(((theirs, swapped), (swapped, theirs))):
        first = jnp.concatenate([zero, zero, a, zero, zero, zero, zero], axis=0)
        second = jnp.concatenate([zero, b, zero, zero, zero, zero, zero], axis=0)
        both = jnp.where(low, first, second).astype(jnp.bfloat16)
        rows = both.shape[0]
        w_ref[w * PAD : w * PAD + rows, 0:128] = both
        w_ref[w * PAD + rows : (w + 1) * PAD, 0:128] = jnp.zeros((PAD - rows, 128), jnp.bfloat16)
        w_ref[w * PAD : w * PAD + rows - 32, 128:256] = both[32:]
        w_ref[w * PAD + rows - 32 : (w + 1) * PAD, 128:256] = jnp.zeros((PAD - rows + 32, 128), jnp.bfloat16)


def correlate(places, theirs, lhs_ref, out_refs, w_ref):
    fill_weights(theirs, w_ref)
    weights = w_ref[...]
    half = lhs_ref.shape[0] // 2
    size = lhs_ref.shape[0] // len(places)
    for base in (half, 0):
        part = jnp.dot(lhs_ref[base : base + half, :], weights, preferred_element_type=jnp.float32)
        for place, (index, at) in enumerate(places):
            row = place * size - base
            if 0 <= row < half:
                ref = out_refs[index]
                ref[at * size : (at + 1) * size, :] = part[row : row + size].astype(ref.dtype)


def paired_kernel(theirs_ref, lhs_ref, theirs2_ref, lhs2_ref, kept_ref, sent_ref, w_ref, sum_ref):
    half = lhs2_ref.shape[0]
    fill_weights(theirs_ref[...], w_ref)
    sum_ref[...] = jnp.dot(lhs_ref[0:half, :], w_ref[...], preferred_element_type=jnp.float32)
    fill_weights(theirs2_ref[...], w_ref)
    total = sum_ref[...] + jnp.dot(lhs2_ref[...], w_ref[...], preferred_element_type=jnp.float32)
    size = kept_ref.shape[0]
    kept_ref[...] = total[0:size]
    sent_ref[...] = total[size:].astype(jnp.bfloat16)


def known_kernel(places, theirs_ref, lhs_ref, *refs):
    correlate(places, theirs_ref[...], lhs_ref, refs[:-1], refs[-1])


def third_mask(masks_ref, last):
    return masks_ref[0] ^ masks_ref[1] ^ masks_ref[2] ^ 1 ^ last


def other_core(third):
    return (third == 3) | (third == 5)


def passed_kernel(last, masks_ref, white_ref, near_ref, out_ref):
    flip = other_core(third_mask(masks_ref, last))

    @pl.when(flip)
    def _():
        out_ref[...] = near_ref[...]

    @pl.when(jnp.logical_not(flip))
    def _():
        out_ref[...] = white_ref[...]


def chosen_kernel(places, last, masks_ref, x_ref, y_ref, corner_ref, lhs_ref, *refs):
    outs, w_ref = refs[:-1], refs[-1]
    masks = masks_ref[...]
    chip = (masks[:, 0:1] ^ masks[:, 1:2] ^ masks[:, 2:3] ^ 1 ^ last) >> 1
    x, y, corner = (ref[...].astype(jnp.float32) for ref in (x_ref, y_ref, corner_ref))
    theirs = jnp.where(chip == 1, x, jnp.where(chip == 2, y, corner))
    correlate(places, theirs, lhs_ref, outs, w_ref)


def finish_kernel(share, norm, last, names, counts, masks_hbm, *refs):
    ins, out_ref, s_ref, plane_ref, masks_ref, sems = list(refs[: sum(counts)]), *refs[-5:]
    fetch = pltpu.make_async_copy(masks_hbm, masks_ref, sems.at[len(names)])
    fetch.start()
    low = lax.broadcasted_iota(jnp.int32, (1, 128), 1) < 64
    rows = PLANES * share
    copies = []
    for k, name in enumerate(names):
        total = sum(ins.pop(0)[0:rows, :].astype(jnp.float32) for _ in range(counts[k])) * norm
        s_ref[0] = total[:, 0:128]
        s_ref[1] = total[:, 128:256]
        for pair in range(share // 2):
            to = slice(pair * 128, pair * 128 + 128)
            for tile in range(COARSE // 2):
                one = s_ref[tile, pl.ds(2 * pair, FINE, stride=share), :]
                two = s_ref[tile, pl.ds(2 * pair + 1, FINE, stride=share), :]
                q = 2 * tile * FINE
                plane_ref[k, q : q + FINE, to] = jnp.where(low, one, pltpu.roll(two, 64, 1))
                plane_ref[k, q + FINE : q + 2 * FINE, to] = jnp.where(low, pltpu.roll(one, 64, 1), two)
            one = s_ref[1, FINE * share + 2 * pair : FINE * share + 2 * pair + 1, :]
            two = s_ref[1, FINE * share + 2 * pair + 1 : FINE * share + 2 * pair + 2, :]
            plane_ref[k, LAGS - 1 : LAGS, to] = jnp.where(low, pltpu.roll(one, 64, 1), two)
        if k == 0:
            fetch.wait()
        mask = {"near": 1, "far": last, "third": third_mask(masks_ref, last)}[name]
        r = jnp.where(masks_ref[0] == mask, 0, jnp.where(masks_ref[1] == mask, 1, 2))
        copies.append(pltpu.make_async_copy(plane_ref.at[k], out_ref.at[r], sems.at[k]))
        copies[-1].start()
    for copy in copies:
        copy.wait()


def apart(value, axis, mask):
    return lax.ppermute(value, axis, [(s, s ^ mask) for s in range(lax.axis_size(axis))])


def local(records, filter_taps, window_offsets, pair_masks):
    chans, rec_len = records.shape[1], records.shape[2]
    taps = filter_taps.shape[0]
    blocks = lax.axis_size("chan")
    days = lax.axis_size("day")
    share = chans // days
    last = blocks - 1
    bf16, f32 = jnp.bfloat16, jnp.float32
    white = call(
        whiten_kernel,
        jax.ShapeDtypeStruct((L, 2 * chans), bf16),
        [HBM] * 3,
        [
            pltpu.SMEM((1, 2), jnp.int32),
            pltpu.VMEM((1, taps), bf16),
            pltpu.VMEM((1, chans, rec_len), bf16),
            pltpu.VMEM((2, 2 * chans, CUT), bf16),
            pltpu.SemaphoreType.DMA((3,)),
        ],
        micros=2.0,
        vmem=63,
    )(window_offsets, filter_taps.reshape(1, -1), records)

    near = apart(white, "chan", 1)
    far = apart(white, "chan", last)
    if days == 4:
        white2 = apart(lax.optimization_barrier((white, near))[0] if LATE_Z else white, "day", 1)

    def prepare(block, count):
        return call(
            functools.partial(prepare_kernel, days, count),
            jax.ShapeDtypeStruct((PLANES * share * count, 2 * PAD), bf16),
            [VMEM],
            micros=1.5,
        )(block)

    lhs = prepare(lax.optimization_barrier((white, near))[0] if EARLY else white, days)

    slot_rows = PLANES * share
    weights = pltpu.VMEM((2 * PAD, 256), bf16)

    def reverse(slot):
        return sum(((slot >> b) & 1) << (days.bit_length() - 2 - b) for b in range(days.bit_length() - 1))

    def plan(mode):
        if mode == "direct":
            return list(DIRECT_ORDER), [([slot], bf16 if slot else f32) for slot in range(days)]
        steps = [1 << b for b in range(days.bit_length() - 1)]
        if mode == "high":
            steps = steps[::-1]
        left, outs = list(range(days)), []
        for step in steps:
            outs.insert(0, ([slot for slot in left if slot & step], bf16 if len(left) == days else f32))
            left = [slot for slot in left if not slot & step]
        return steps, [(left, f32)] + outs

    def started(mode, steps, outs, parts):
        if mode == "direct":
            came = [parts[0]] + [apart(parts[s], "day", s) for s in steps]
            return lambda after=None: came
        kept = list(parts[:-1])
        came = [apart(parts[-1], "day", steps[0])]
        held = [[slot ^ steps[0] for slot in outs[-1][0]]]

        def rest(after=None):
            if after is not None:
                came[0], _ = lax.optimization_barrier((came[0], after))
            for step in steps[1:]:
                piece, slots = kept.pop(), outs[len(kept)][0]
                n = piece.shape[0]
                for c, slots_c in zip(came, held):
                    at = slots_c.index(slots[0]) * slot_rows
                    piece = piece + c[at : at + n].astype(f32)
                held.append([slot ^ step for slot in slots])
                came.append(apart(piece.astype(bf16), "day", step))
            return [kept[0]] + came

        rest.came = came
        return rest

    def day_sum(mode, theirs, pick=None):
        mode = mode if days == 4 else "low"
        steps, outs = plan(mode)
        shapes = [jax.ShapeDtypeStruct((len(slots) * slot_rows, 256), kind) for slots, kind in outs]
        where = {slot: (k, at) for k, (slots, _) in enumerate(outs) for at, slot in enumerate(slots)}
        places = [where[reverse(place)] for place in range(days)]
        if pick is None:
            parts = call(functools.partial(known_kernel, places), shapes, [VMEM] * 2, [weights], micros=2.0)(theirs, lhs)
        else:
            parts = call(
                functools.partial(chosen_kernel, places, last),
                shapes,
                [VMEM] * (len(theirs) + 2),
                [weights],
                micros=2.0,
            )(pick.reshape(1, -1), *theirs, lhs)
        return parts[-1], started(mode, steps, outs, parts)

    if blocks == 8:
        passed = call(
            functools.partial(passed_kernel, last),
            jax.ShapeDtypeStruct(white.shape, bf16),
            [SMEM] + [VMEM] * 2,
            micros=0.5,
        )(pair_masks, white, near)
        along_x = apart(passed, "chan", 2)
        along_y = apart(passed, "chan", 4)
    far_done, far_sum = day_sum(FAR, far)
    if days == 4:
        if FAR_FIRST:
            white2, _ = lax.optimization_barrier((white2, far_done))
        near2 = apart(white2, "chan", 1)
        near_kept, near_done = call(
            paired_kernel,
            [jax.ShapeDtypeStruct((slot_rows, 256), f32), jax.ShapeDtypeStruct((slot_rows, 256), bf16)],
            [VMEM] * 4,
            [weights, pltpu.VMEM((2 * slot_rows, 256), f32)],
            micros=2.0,
        )(near, lhs, near2, prepare(white2, 2))
        near_came = [near_kept, apart(near_done, "day", 2)]
    else:
        near_done, near_sum = day_sum("low", near)
        near_came = near_sum()
    if blocks == 8:
        corner = apart(far, "chan", 1)
        if NEAR_FIRST:
            along_x, along_y, _ = lax.optimization_barrier((along_x, along_y, near_done))
        free_done, free_sum = day_sum(FREE, (along_x, along_y, corner), pair_masks)
    else:
        free = white
        third = pair_masks[0] ^ pair_masks[1] ^ pair_masks[2] ^ 1 ^ last
        for bit in range(blocks.bit_length() - 1):
            free = jnp.where(((third >> bit) & 1) == 1, apart(free, "chan", 2**bit), free)
        free_done, free_sum = day_sum(FREE, free)
    far_came = far_sum(free_done if FAR_AFTER else None)
    sums = [near_came, far_came, free_sum((None, near_came[-1], (near_came[-1], far_came[-1]))[LAST_AFTER])]

    day_total = records.shape[0] * days
    norm = float((day_total * window_offsets.shape[1] * L) ** -0.5)

    def finish(names, groups, before=None):
        flat = [part for group in groups for part in group]
        extra = [] if before is None else [before]
        return pl.pallas_call(
            functools.partial(finish_kernel, share, norm, last, names, [len(group) for group in groups]),
            out_shape=jax.ShapeDtypeStruct((3, LAGS, share * chans), f32),
            in_specs=[HBM] + [VMEM] * len(flat) + [HBM] * len(extra),
            out_specs=HBM,
            scratch_shapes=[
                pltpu.VMEM((2, slot_rows, 128), f32),
                pltpu.VMEM((len(names), LAGS, share * chans), f32),
                pltpu.SMEM(pair_masks.shape, jnp.int32),
                pltpu.SemaphoreType.DMA((len(names) + 1,)),
            ],
            input_output_aliases={1 + len(flat): 0} if extra else {},
            compiler_params=pltpu.CompilerParams(vmem_limit_bytes=24 * 1024 * 1024),
            cost_estimate=pl.CostEstimate(flops=int(1e9), bytes_accessed=int(3e6), transcendentals=0),
        )(pair_masks, *flat, *extra)

    return finish(["third"], sums[2:], finish(["near", "far"], sums[:2]))


def solution(mesh):
    in_specs = (P("day", "chan", None), P(), P("day", None), P())
    out_specs = P(None, None, ("chan", "day"))
    return jax.shard_map(local, mesh=mesh, in_specs=in_specs, out_specs=out_specs, check_vma=False)
```

```python
import functools

import jax
import jax.numpy as jnp
from jax import lax
from jax.experimental import pallas as pl
from jax.experimental.pallas import tpu as pltpu
from jax.sharding import PartitionSpec as P

L = 1024
MAXLAG = 32
LAGS = 2 * MAXLAG + 1
FINE = 16
COARSE = 4
PLANES = FINE + 1
PAD = 1152
CUT = 1280
COST = 3.0
DIRECT_ORDER = (2, 3, 1)
FAR_AFTER = False
LAST_AFTER = 1
LATE_Z = False
FAR_FIRST = True
EARLY = False
NEAR_FIRST = False
FAR, FREE = "low", "low"
NT = (((1,), (1,)), ((), ()))
VMEM = pl.BlockSpec(memory_space=pltpu.VMEM)
SMEM = pl.BlockSpec(memory_space=pltpu.SMEM)
HBM = pl.BlockSpec(memory_space=pltpu.HBM)


def call(kernel, out_shape, in_specs, scratch=(), micros=1.0, vmem=24):
    many = isinstance(out_shape, list)
    return pl.pallas_call(
        kernel,
        out_shape=out_shape,
        in_specs=in_specs,
        out_specs=[VMEM] * len(out_shape) if many else VMEM,
        scratch_shapes=list(scratch),
        compiler_params=pltpu.CompilerParams(vmem_limit_bytes=vmem * 1024 * 1024),
        cost_estimate=pl.CostEstimate(flops=int(micros * COST * 1e9), bytes_accessed=int(micros * COST * 3e6), transcendentals=0),
    )


def whiten_kernel(off_hbm, taps_hbm, rec_hbm, out_ref, off_ref, taps_ref, rec_ref, wide_ref, sems):
    copies = [
        pltpu.make_async_copy(src, dst, sems.at[k])
        for k, (src, dst) in enumerate(((off_hbm, off_ref), (rec_hbm, rec_ref), (taps_hbm, taps_ref)))
    ]
    for copy in copies:
        copy.start()
    chans, rec_len = rec_ref.shape[1], rec_ref.shape[2]
    wide_ref[...] = jnp.zeros_like(wide_ref)
    copies[2].wait()
    copies[0].wait()
    taps = taps_ref[...].astype(jnp.float32)
    row = jnp.concatenate([taps, jnp.zeros((1, 384 - taps.shape[1]), jnp.float32)], axis=1)
    row = jnp.broadcast_to(row, (8, 384))
    bands, bases = [], []
    for w in range(2):
        start = off_ref[0, w]
        base = jnp.minimum((start // 128) * 128, rec_len - CUT)
        bases.append(pl.multiple_of(base, 128))
        moved = pltpu.roll(row, start - base, 1)
        block = jnp.broadcast_to(moved[0:1], (128, 384))
        block = pltpu.roll(block, 0, 1, stride=1, stride_axis=0).astype(jnp.bfloat16)
        none = jnp.zeros((128, 128), jnp.bfloat16)
        bands.append(
            jnp.concatenate(
                [jnp.concatenate([block, none], axis=1), jnp.concatenate([none, block], axis=1)],
                axis=0,
            )
        )
    copies[1].wait()
    for w in range(2):
        wide_ref[w, w * chans : (w + 1) * chans, :] = rec_ref[0, :, pl.ds(bases[w], CUT)]
    parts = []
    for c in range(0, L, 512):
        pair = 0.0
        for w in range(2):
            both = jnp.concatenate([wide_ref[w, :, c : c + 512], wide_ref[w, :, c + 256 : c + 768]], axis=0)
            pair += lax.dot_general(bands[w], both, NT, preferred_element_type=jnp.float32)
        parts += [pair[:, 0:128], pair[:, 128:256]]
    power = sum(jnp.sum(part * part, axis=0, keepdims=True) for part in parts) * (1.0 / L)
    scale = lax.rsqrt(power + 1e-06)
    for c, part in enumerate(parts):
        out_ref[c * 256 : (c + 1) * 256, :] = (part * scale).astype(jnp.bfloat16)


def prepare_kernel(days, count, white_ref, lhs_ref):
    chans = white_ref.shape[1] // 2
    share = chans // days
    bits = days.bit_length() - 1
    me = lax.axis_index("day")
    rows = lax.broadcasted_iota(jnp.int32, (2 * chans, 2 * chans), 0)
    cols = lax.broadcasted_iota(jnp.int32, (2 * chans, 2 * chans), 1)
    place = (rows % chans) // share
    slot = jnp.zeros_like(place)
    for b in range(bits):
        slot = slot + (((place >> b) & 1) << (bits - 1 - b))
    source = (rows // chans) * chans + (slot ^ me) * share + rows % share
    pick = (cols == source).astype(jnp.float32).astype(jnp.bfloat16)
    mine = lax.dot_general(pick, white_ref[...], NT, preferred_element_type=jnp.float32)
    mine = jnp.concatenate([mine, jnp.zeros((2 * chans, PAD - L), jnp.float32)], axis=1)
    for p in range(PLANES):
        moved = (pltpu.roll(mine, p, 1) if p else mine).astype(jnp.bfloat16)
        for w in range(2):
            for b in range(count):
                at = (b * PLANES + p) * share
                lhs_ref[at : at + share, w * PAD : (w + 1) * PAD] = moved[w * chans + b * share : w * chans + (b + 1) * share]


def fill_weights(theirs, w_ref):
    theirs = theirs.astype(jnp.float32)
    swapped = pltpu.roll(theirs, 64, 1)
    low = lax.broadcasted_iota(jnp.int32, (1, 128), 1) < 64
    zero = jnp.zeros((16, 128), jnp.float32)
    for w, (a, b) in enumerate(((theirs, swapped), (swapped, theirs))):
        first = jnp.concatenate([zero, zero, a, zero, zero, zero, zero], axis=0)
        second = jnp.concatenate([zero, b, zero, zero, zero, zero, zero], axis=0)
        both = jnp.where(low, first, second).astype(jnp.bfloat16)
        rows = both.shape[0]
        w_ref[w * PAD : w * PAD + rows, 0:128] = both
        w_ref[w * PAD + rows : (w + 1) * PAD, 0:128] = jnp.zeros((PAD - rows, 128), jnp.bfloat16)
        w_ref[w * PAD : w * PAD + rows - 32, 128:256] = both[32:]
        w_ref[w * PAD + rows - 32 : (w + 1) * PAD, 128:256] = jnp.zeros((PAD - rows + 32, 128), jnp.bfloat16)


def correlate(places, theirs, lhs_ref, out_refs, w_ref):
    fill_weights(theirs, w_ref)
    weights = w_ref[...]
    half = lhs_ref.shape[0] // 2
    size = lhs_ref.shape[0] // len(places)
    for base in (half, 0):
        part = jnp.dot(lhs_ref[base : base + half, :], weights, preferred_element_type=jnp.float32)
        for place, (index, at) in enumerate(places):
            row = place * size - base
            if 0 <= row < half:
                ref = out_refs[index]
                ref[at * size : (at + 1) * size, :] = part[row : row + size].astype(ref.dtype)


def paired_kernel(theirs_ref, lhs_ref, theirs2_ref, lhs2_ref, kept_ref, sent_ref, w_ref, sum_ref):
    half = lhs2_ref.shape[0]
    fill_weights(theirs_ref[...], w_ref)
    sum_ref[...] = jnp.dot(lhs_ref[0:half, :], w_ref[...], preferred_element_type=jnp.float32)
    fill_weights(theirs2_ref[...], w_ref)
    total = sum_ref[...] + jnp.dot(lhs2_ref[...], w_ref[...], preferred_element_type=jnp.float32)
    size = kept_ref.shape[0]
    kept_ref[...] = total[0:size]
    sent_ref[...] = total[size:].astype(jnp.bfloat16)


def known_kernel(places, theirs_ref, lhs_ref, *refs):
    correlate(places, theirs_ref[...], lhs_ref, refs[:-1], refs[-1])


def third_mask(masks_ref, last):
    return masks_ref[0] ^ masks_ref[1] ^ masks_ref[2] ^ 1 ^ last


def other_core(third):
    return (third == 3) | (third == 5)


def passed_kernel(last, masks_ref, white_ref, near_ref, out_ref):
    flip = other_core(third_mask(masks_ref, last))

    @pl.when(flip)
    def _():
        out_ref[...] = near_ref[...]

    @pl.when(jnp.logical_not(flip))
    def _():
        out_ref[...] = white_ref[...]


def chosen_kernel(places, last, masks_ref, x_ref, y_ref, corner_ref, lhs_ref, *refs):
    outs, w_ref = refs[:-1], refs[-1]
    masks = masks_ref[...]
    chip = (masks[:, 0:1] ^ masks[:, 1:2] ^ masks[:, 2:3] ^ 1 ^ last) >> 1
    x, y, corner = (ref[...].astype(jnp.float32) for ref in (x_ref, y_ref, corner_ref))
    theirs = jnp.where(chip == 1, x, jnp.where(chip == 2, y, corner))
    correlate(places, theirs, lhs_ref, outs, w_ref)


def finish_kernel(share, norm, last, names, counts, masks_hbm, *refs):
    ins, out_ref, s_ref, plane_ref, masks_ref, sems = list(refs[: sum(counts)]), *refs[-5:]
    fetch = pltpu.make_async_copy(masks_hbm, masks_ref, sems.at[len(names)])
    fetch.start()
    low = lax.broadcasted_iota(jnp.int32, (1, 128), 1) < 64
    rows = PLANES * share
    copies = []
    for k, name in enumerate(names):
        total = sum(ins.pop(0)[0:rows, :].astype(jnp.float32) for _ in range(counts[k])) * norm
        s_ref[0] = total[:, 0:128]
        s_ref[1] = total[:, 128:256]
        for pair in range(share // 2):
            to = slice(pair * 128, pair * 128 + 128)
            for tile in range(COARSE // 2):
                one = s_ref[tile, pl.ds(2 * pair, FINE, stride=share), :]
                two = s_ref[tile, pl.ds(2 * pair + 1, FINE, stride=share), :]
                q = 2 * tile * FINE
                plane_ref[k, q : q + FINE, to] = jnp.where(low, one, pltpu.roll(two, 64, 1))
                plane_ref[k, q + FINE : q + 2 * FINE, to] = jnp.where(low, pltpu.roll(one, 64, 1), two)
            one = s_ref[1, FINE * share + 2 * pair : FINE * share + 2 * pair + 1, :]
            two = s_ref[1, FINE * share + 2 * pair + 1 : FINE * share + 2 * pair + 2, :]
            plane_ref[k, LAGS - 1 : LAGS, to] = jnp.where(low, pltpu.roll(one, 64, 1), two)
        if k == 0:
            fetch.wait()
        mask = {"near": 1, "far": last, "third": third_mask(masks_ref, last)}[name]
        r = jnp.where(masks_ref[0] == mask, 0, jnp.where(masks_ref[1] == mask, 1, 2))
        copies.append(pltpu.make_async_copy(plane_ref.at[k], out_ref.at[r], sems.at[k]))
        copies[-1].start()
    for copy in copies:
        copy.wait()


def apart(value, axis, mask):
    return lax.ppermute(value, axis, [(s, s ^ mask) for s in range(lax.axis_size(axis))])


def local(records, filter_taps, window_offsets, pair_masks):
    chans, rec_len = records.shape[1], records.shape[2]
    taps = filter_taps.shape[0]
    blocks = lax.axis_size("chan")
    days = lax.axis_size("day")
    share = chans // days
    last = blocks - 1
    bf16, f32 = jnp.bfloat16, jnp.float32
    white = call(
        whiten_kernel,
        jax.ShapeDtypeStruct((L, 2 * chans), bf16),
        [HBM] * 3,
        [
            pltpu.SMEM((1, 2), jnp.int32),
            pltpu.VMEM((1, taps), bf16),
            pltpu.VMEM((1, chans, rec_len), bf16),
            pltpu.VMEM((2, 2 * chans, CUT), bf16),
            pltpu.SemaphoreType.DMA((3,)),
        ],
        micros=2.0,
        vmem=63,
    )(window_offsets, filter_taps.reshape(1, -1), records)

    near = apart(white, "chan", 1)
    far = apart(white, "chan", last)
    if days == 4:
        white2 = apart(lax.optimization_barrier((white, near))[0] if LATE_Z else white, "day", 1)

    def prepare(block, count):
        return call(
            functools.partial(prepare_kernel, days, count),
            jax.ShapeDtypeStruct((PLANES * share * count, 2 * PAD), bf16),
            [VMEM],
            micros=1.5,
        )(block)

    lhs = prepare(lax.optimization_barrier((white, near))[0] if EARLY else white, days)

    slot_rows = PLANES * share
    weights = pltpu.VMEM((2 * PAD, 256), bf16)

    def reverse(slot):
        return sum(((slot >> b) & 1) << (days.bit_length() - 2 - b) for b in range(days.bit_length() - 1))

    def plan(mode):
        if mode == "direct":
            return list(DIRECT_ORDER), [([slot], bf16 if slot else f32) for slot in range(days)]
        steps = [1 << b for b in range(days.bit_length() - 1)]
        if mode == "high":
            steps = steps[::-1]
        left, outs = list(range(days)), []
        for step in steps:
            outs.insert(0, ([slot for slot in left if slot & step], bf16 if len(left) == days else f32))
            left = [slot for slot in left if not slot & step]
        return steps, [(left, f32)] + outs

    def started(mode, steps, outs, parts):
        if mode == "direct":
            came = [parts[0]] + [apart(parts[s], "day", s) for s in steps]
            return lambda after=None: came
        kept = list(parts[:-1])
        came = [apart(parts[-1], "day", steps[0])]
        held = [[slot ^ steps[0] for slot in outs[-1][0]]]

        def rest(after=None):
            if after is not None:
                came[0], _ = lax.optimization_barrier((came[0], after))
            for step in steps[1:]:
                piece, slots = kept.pop(), outs[len(kept)][0]
                n = piece.shape[0]
                for c, slots_c in zip(came, held):
                    at = slots_c.index(slots[0]) * slot_rows
                    piece = piece + c[at : at + n].astype(f32)
                held.append([slot ^ step for slot in slots])
                came.append(apart(piece.astype(bf16), "day", step))
            return [kept[0]] + came

        rest.came = came
        return rest

    def day_sum(mode, theirs, pick=None):
        mode = mode if days == 4 else "low"
        steps, outs = plan(mode)
        shapes = [jax.ShapeDtypeStruct((len(slots) * slot_rows, 256), kind) for slots, kind in outs]
        where = {slot: (k, at) for k, (slots, _) in enumerate(outs) for at, slot in enumerate(slots)}
        places = [where[reverse(place)] for place in range(days)]
        if pick is None:
            parts = call(functools.partial(known_kernel, places), shapes, [VMEM] * 2, [weights], micros=2.0)(theirs, lhs)
        else:
            parts = call(
                functools.partial(chosen_kernel, places, last),
                shapes,
                [VMEM] * (len(theirs) + 2),
                [weights],
                micros=2.0,
            )(pick.reshape(1, -1), *theirs, lhs)
        return parts[-1], started(mode, steps, outs, parts)

    if blocks == 8:
        passed = call(
            functools.partial(passed_kernel, last),
            jax.ShapeDtypeStruct(white.shape, bf16),
            [SMEM] + [VMEM] * 2,
            micros=0.5,
        )(pair_masks, white, near)
        along_x = apart(passed, "chan", 2)
        along_y = apart(passed, "chan", 4)
    far_done, far_sum = day_sum(FAR, far)
    if days == 4:
        if FAR_FIRST:
            white2, _ = lax.optimization_barrier((white2, far_done))
        near2 = apart(white2, "chan", 1)
        near_kept, near_done = call(
            paired_kernel,
            [jax.ShapeDtypeStruct((slot_rows, 256), f32), jax.ShapeDtypeStruct((slot_rows, 256), bf16)],
            [VMEM] * 4,
            [weights, pltpu.VMEM((2 * slot_rows, 256), f32)],
            micros=2.0,
        )(near, lhs, near2, prepare(white2, 2))
        near_came = [near_kept, apart(near_done, "day", 2)]
    else:
        near_done, near_sum = day_sum("low", near)
        near_came = near_sum()
    if blocks == 8:
        corner = apart(far, "chan", 1)
        if NEAR_FIRST:
            along_x, along_y, _ = lax.optimization_barrier((along_x, along_y, near_done))
        free_done, free_sum = day_sum(FREE, (along_x, along_y, corner), pair_masks)
    else:
        free = white
        third = pair_masks[0] ^ pair_masks[1] ^ pair_masks[2] ^ 1 ^ last
        for bit in range(blocks.bit_length() - 1):
            free = jnp.where(((third >> bit) & 1) == 1, apart(free, "chan", 2**bit), free)
        free_done, free_sum = day_sum(FREE, free)
    far_came = far_sum(free_done if FAR_AFTER else None)
    sums = [near_came, far_came, free_sum((None, near_came[-1], (near_came[-1], far_came[-1]))[LAST_AFTER])]

    day_total = records.shape[0] * days
    norm = float((day_total * window_offsets.shape[1] * L) ** -0.5)

    def finish(names, groups, before=None):
        flat = [part for group in groups for part in group]
        extra = [] if before is None else [before]
        return pl.pallas_call(
            functools.partial(finish_kernel, share, norm, last, names, [len(group) for group in groups]),
            out_shape=jax.ShapeDtypeStruct((3, LAGS, share * chans), f32),
            in_specs=[HBM] + [VMEM] * len(flat) + [HBM] * len(extra),
            out_specs=HBM,
            scratch_shapes=[
                pltpu.VMEM((2, slot_rows, 128), f32),
                pltpu.VMEM((len(names), LAGS, share * chans), f32),
                pltpu.SMEM(pair_masks.shape, jnp.int32),
                pltpu.SemaphoreType.DMA((len(names) + 1,)),
            ],
            input_output_aliases={1 + len(flat): 0} if extra else {},
            compiler_params=pltpu.CompilerParams(vmem_limit_bytes=24 * 1024 * 1024),
            cost_estimate=pl.CostEstimate(flops=int(1e9), bytes_accessed=int(3e6), transcendentals=0),
        )(pair_masks, *flat, *extra)

    return finish(["third"], sums[2:], finish(["near", "far"], sums[:2]))


def solution(mesh):
    in_specs = (P("day", "chan", None), P(), P("day", None), P())
    out_specs = P(None, None, ("chan", "day"))
    return jax.shard_map(local, mesh=mesh, in_specs=in_specs, out_specs=out_specs, check_vma=False)
```

```python
import functools

import jax
import jax.numpy as jnp
from jax import lax
from jax.experimental import pallas as pl
from jax.experimental.pallas import tpu as pltpu
from jax.sharding import PartitionSpec as P

L = 1024
MAXLAG = 32
LAGS = 2 * MAXLAG + 1
FINE = 16
COARSE = 4
PLANES = FINE + 1
PAD = 1152
CUT = 1280
COST = 3.0
DIRECT_ORDER = (2, 3, 1)
FAR_AFTER = False
LAST_AFTER = 1
LATE_Z = False
FAR_FIRST = True
EARLY = False
NEAR_FIRST = False
FAR, FREE = "low", "low"
NT = (((1,), (1,)), ((), ()))
VMEM = pl.BlockSpec(memory_space=pltpu.VMEM)
SMEM = pl.BlockSpec(memory_space=pltpu.SMEM)
HBM = pl.BlockSpec(memory_space=pltpu.HBM)


def call(kernel, out_shape, in_specs, scratch=(), micros=1.0, vmem=24):
    many = isinstance(out_shape, list)
    return pl.pallas_call(
        kernel,
        out_shape=out_shape,
        in_specs=in_specs,
        out_specs=[VMEM] * len(out_shape) if many else VMEM,
        scratch_shapes=list(scratch),
        compiler_params=pltpu.CompilerParams(vmem_limit_bytes=vmem * 1024 * 1024),
        cost_estimate=pl.CostEstimate(flops=int(micros * COST * 1e9), bytes_accessed=int(micros * COST * 3e6), transcendentals=0),
    )


def whiten_kernel(off_hbm, taps_hbm, rec_hbm, out_ref, off_ref, taps_ref, rec_ref, wide_ref, sems):
    copies = [
        pltpu.make_async_copy(src, dst, sems.at[k])
        for k, (src, dst) in enumerate(((off_hbm, off_ref), (rec_hbm, rec_ref), (taps_hbm, taps_ref)))
    ]
    for copy in copies:
        copy.start()
    chans, rec_len = rec_ref.shape[1], rec_ref.shape[2]
    wide_ref[...] = jnp.zeros_like(wide_ref)
    copies[2].wait()
    copies[0].wait()
    taps = taps_ref[...].astype(jnp.float32)
    row = jnp.concatenate([taps, jnp.zeros((1, 384 - taps.shape[1]), jnp.float32)], axis=1)
    row = jnp.broadcast_to(row, (8, 384))
    bands, bases = [], []
    for w in range(2):
        start = off_ref[0, w]
        base = jnp.minimum((start // 128) * 128, rec_len - CUT)
        bases.append(pl.multiple_of(base, 128))
        moved = pltpu.roll(row, start - base, 1)
        block = jnp.broadcast_to(moved[0:1], (128, 384))
        block = pltpu.roll(block, 0, 1, stride=1, stride_axis=0).astype(jnp.bfloat16)
        none = jnp.zeros((128, 128), jnp.bfloat16)
        bands.append(
            jnp.concatenate(
                [jnp.concatenate([block, none], axis=1), jnp.concatenate([none, block], axis=1)],
                axis=0,
            )
        )
    copies[1].wait()
    for w in range(2):
        wide_ref[w, w * chans : (w + 1) * chans, :] = rec_ref[0, :, pl.ds(bases[w], CUT)]
    parts = []
    for c in range(0, L, 512):
        pair = 0.0
        for w in range(2):
            both = jnp.concatenate([wide_ref[w, :, c : c + 512], wide_ref[w, :, c + 256 : c + 768]], axis=0)
            pair += lax.dot_general(bands[w], both, NT, preferred_element_type=jnp.float32)
        parts += [pair[:, 0:128], pair[:, 128:256]]
    power = sum(jnp.sum(part * part, axis=0, keepdims=True) for part in parts) * (1.0 / L)
    scale = lax.rsqrt(power + 1e-06)
    for c, part in enumerate(parts):
        out_ref[c * 256 : (c + 1) * 256, :] = (part * scale).astype(jnp.bfloat16)


def prepare_kernel(days, count, white_ref, lhs_ref):
    chans = white_ref.shape[1] // 2
    share = chans // days
    bits = days.bit_length() - 1
    me = lax.axis_index("day")
    rows = lax.broadcasted_iota(jnp.int32, (2 * chans, 2 * chans), 0)
    cols = lax.broadcasted_iota(jnp.int32, (2 * chans, 2 * chans), 1)
    place = (rows % chans) // share
    slot = jnp.zeros_like(place)
    for b in range(bits):
        slot = slot + (((place >> b) & 1) << (bits - 1 - b))
    source = (rows // chans) * chans + (slot ^ me) * share + rows % share
    pick = (cols == source).astype(jnp.float32).astype(jnp.bfloat16)
    mine = lax.dot_general(pick, white_ref[...], NT, preferred_element_type=jnp.float32)
    mine = jnp.concatenate([mine, jnp.zeros((2 * chans, PAD - L), jnp.float32)], axis=1)
    for p in range(PLANES):
        moved = (pltpu.roll(mine, p, 1) if p else mine).astype(jnp.bfloat16)
        for w in range(2):
            for b in range(count):
                at = (b * PLANES + p) * share
                lhs_ref[at : at + share, w * PAD : (w + 1) * PAD] = moved[w * chans + b * share : w * chans + (b + 1) * share]


def fill_weights(theirs, w_ref):
    theirs = theirs.astype(jnp.float32)
    swapped = pltpu.roll(theirs, 64, 1)
    low = lax.broadcasted_iota(jnp.int32, (1, 128), 1) < 64
    zero = jnp.zeros((16, 128), jnp.float32)
    for w, (a, b) in enumerate(((theirs, swapped), (swapped, theirs))):
        first = jnp.concatenate([zero, zero, a, zero, zero, zero, zero], axis=0)
        second = jnp.concatenate([zero, b, zero, zero, zero, zero, zero], axis=0)
        both = jnp.where(low, first, second).astype(jnp.bfloat16)
        rows = both.shape[0]
        w_ref[w * PAD : w * PAD + rows, 0:128] = both
        w_ref[w * PAD + rows : (w + 1) * PAD, 0:128] = jnp.zeros((PAD - rows, 128), jnp.bfloat16)
        w_ref[w * PAD : w * PAD + rows - 32, 128:256] = both[32:]
        w_ref[w * PAD + rows - 32 : (w + 1) * PAD, 128:256] = jnp.zeros((PAD - rows + 32, 128), jnp.bfloat16)


def correlate(places, theirs, lhs_ref, out_refs, w_ref):
    fill_weights(theirs, w_ref)
    weights = w_ref[...]
    half = lhs_ref.shape[0] // 2
    size = lhs_ref.shape[0] // len(places)
    for base in (half, 0):
        part = jnp.dot(lhs_ref[base : base + half, :], weights, preferred_element_type=jnp.float32)
        for place, (index, at) in enumerate(places):
            row = place * size - base
            if 0 <= row < half:
                ref = out_refs[index]
                ref[at * size : (at + 1) * size, :] = part[row : row + size].astype(ref.dtype)


def paired_kernel(theirs_ref, lhs_ref, theirs2_ref, lhs2_ref, kept_ref, sent_ref, w_ref, sum_ref):
    half = lhs2_ref.shape[0]
    fill_weights(theirs_ref[...], w_ref)
    sum_ref[...] = jnp.dot(lhs_ref[0:half, :], w_ref[...], preferred_element_type=jnp.float32)
    fill_weights(theirs2_ref[...], w_ref)
    total = sum_ref[...] + jnp.dot(lhs2_ref[...], w_ref[...], preferred_element_type=jnp.float32)
    size = kept_ref.shape[0]
    kept_ref[...] = total[0:size]
    sent_ref[...] = total[size:].astype(jnp.bfloat16)


def known_kernel(places, theirs_ref, lhs_ref, *refs):
    correlate(places, theirs_ref[...], lhs_ref, refs[:-1], refs[-1])


def third_mask(masks_ref, last):
    return masks_ref[0] ^ masks_ref[1] ^ masks_ref[2] ^ 1 ^ last


def other_core(third):
    return (third == 3) | (third == 5)


def passed_kernel(last, masks_ref, white_ref, near_ref, out_ref):
    masks = masks_ref[...]
    third = masks[:, 0:1] ^ masks[:, 1:2] ^ masks[:, 2:3] ^ 1 ^ last
    white, near = white_ref[...].astype(jnp.float32), near_ref[...].astype(jnp.float32)
    out_ref[...] = jnp.where(other_core(third), near, white).astype(jnp.bfloat16)


def chosen_kernel(places, last, masks_ref, x_ref, y_ref, corner_ref, lhs_ref, *refs):
    outs, w_ref = refs[:-1], refs[-1]
    masks = masks_ref[...]
    chip = (masks[:, 0:1] ^ masks[:, 1:2] ^ masks[:, 2:3] ^ 1 ^ last) >> 1
    x, y, corner = (ref[...].astype(jnp.float32) for ref in (x_ref, y_ref, corner_ref))
    theirs = jnp.where(chip == 1, x, jnp.where(chip == 2, y, corner))
    correlate(places, theirs, lhs_ref, outs, w_ref)


def finish_kernel(share, norm, last, names, counts, masks_hbm, *refs):
    ins, out_ref, s_ref, plane_ref, masks_ref, sems = list(refs[: sum(counts)]), *refs[-5:]
    fetch = pltpu.make_async_copy(masks_hbm, masks_ref, sems.at[len(names)])
    fetch.start()
    low = lax.broadcasted_iota(jnp.int32, (1, 128), 1) < 64
    rows = PLANES * share
    copies = []
    for k, name in enumerate(names):
        total = sum(ins.pop(0)[0:rows, :].astype(jnp.float32) for _ in range(counts[k])) * norm
        s_ref[0] = total[:, 0:128]
        s_ref[1] = total[:, 128:256]
        for pair in range(share // 2):
            to = slice(pair * 128, pair * 128 + 128)
            for tile in range(COARSE // 2):
                one = s_ref[tile, pl.ds(2 * pair, FINE, stride=share), :]
                two = s_ref[tile, pl.ds(2 * pair + 1, FINE, stride=share), :]
                q = 2 * tile * FINE
                plane_ref[k, q : q + FINE, to] = jnp.where(low, one, pltpu.roll(two, 64, 1))
                plane_ref[k, q + FINE : q + 2 * FINE, to] = jnp.where(low, pltpu.roll(one, 64, 1), two)
            one = s_ref[1, FINE * share + 2 * pair : FINE * share + 2 * pair + 1, :]
            two = s_ref[1, FINE * share + 2 * pair + 1 : FINE * share + 2 * pair + 2, :]
            plane_ref[k, LAGS - 1 : LAGS, to] = jnp.where(low, pltpu.roll(one, 64, 1), two)
        if k == 0:
            fetch.wait()
        mask = {"near": 1, "far": last, "third": third_mask(masks_ref, last)}[name]
        r = jnp.where(masks_ref[0] == mask, 0, jnp.where(masks_ref[1] == mask, 1, 2))
        copies.append(pltpu.make_async_copy(plane_ref.at[k], out_ref.at[r], sems.at[k]))
        copies[-1].start()
    for copy in copies:
        copy.wait()


def apart(value, axis, mask):
    return lax.ppermute(value, axis, [(s, s ^ mask) for s in range(lax.axis_size(axis))])


def local(records, filter_taps, window_offsets, pair_masks):
    chans, rec_len = records.shape[1], records.shape[2]
    taps = filter_taps.shape[0]
    blocks = lax.axis_size("chan")
    days = lax.axis_size("day")
    share = chans // days
    last = blocks - 1
    bf16, f32 = jnp.bfloat16, jnp.float32
    white = call(
        whiten_kernel,
        jax.ShapeDtypeStruct((L, 2 * chans), bf16),
        [HBM] * 3,
        [
            pltpu.SMEM((1, 2), jnp.int32),
            pltpu.VMEM((1, taps), bf16),
            pltpu.VMEM((1, chans, rec_len), bf16),
            pltpu.VMEM((2, 2 * chans, CUT), bf16),
            pltpu.SemaphoreType.DMA((3,)),
        ],
        micros=2.0,
        vmem=63,
    )(window_offsets, filter_taps.reshape(1, -1), records)

    near = apart(white, "chan", 1)
    far = apart(white, "chan", last)
    if days == 4:
        white2 = apart(lax.optimization_barrier((white, near))[0] if LATE_Z else white, "day", 1)

    def prepare(block, count):
        return call(
            functools.partial(prepare_kernel, days, count),
            jax.ShapeDtypeStruct((PLANES * share * count, 2 * PAD), bf16),
            [VMEM],
            micros=1.5,
        )(block)

    lhs = prepare(lax.optimization_barrier((white, near))[0] if EARLY else white, days)

    slot_rows = PLANES * share
    weights = pltpu.VMEM((2 * PAD, 256), bf16)

    def reverse(slot):
        return sum(((slot >> b) & 1) << (days.bit_length() - 2 - b) for b in range(days.bit_length() - 1))

    def plan(mode):
        if mode == "direct":
            return list(DIRECT_ORDER), [([slot], bf16 if slot else f32) for slot in range(days)]
        steps = [1 << b for b in range(days.bit_length() - 1)]
        if mode == "high":
            steps = steps[::-1]
        left, outs = list(range(days)), []
        for step in steps:
            outs.insert(0, ([slot for slot in left if slot & step], bf16 if len(left) == days else f32))
            left = [slot for slot in left if not slot & step]
        return steps, [(left, f32)] + outs

    def started(mode, steps, outs, parts):
        if mode == "direct":
            came = [parts[0]] + [apart(parts[s], "day", s) for s in steps]
            return lambda after=None: came
        kept = list(parts[:-1])
        came = [apart(parts[-1], "day", steps[0])]
        held = [[slot ^ steps[0] for slot in outs[-1][0]]]

        def rest(after=None):
            if after is not None:
                came[0], _ = lax.optimization_barrier((came[0], after))
            for step in steps[1:]:
                piece, slots = kept.pop(), outs[len(kept)][0]
                n = piece.shape[0]
                for c, slots_c in zip(came, held):
                    at = slots_c.index(slots[0]) * slot_rows
                    piece = piece + c[at : at + n].astype(f32)
                held.append([slot ^ step for slot in slots])
                came.append(apart(piece.astype(bf16), "day", step))
            return [kept[0]] + came

        rest.came = came
        return rest

    def day_sum(mode, theirs, pick=None):
        mode = mode if days == 4 else "low"
        steps, outs = plan(mode)
        shapes = [jax.ShapeDtypeStruct((len(slots) * slot_rows, 256), kind) for slots, kind in outs]
        where = {slot: (k, at) for k, (slots, _) in enumerate(outs) for at, slot in enumerate(slots)}
        places = [where[reverse(place)] for place in range(days)]
        if pick is None:
            parts = call(functools.partial(known_kernel, places), shapes, [VMEM] * 2, [weights], micros=2.0)(theirs, lhs)
        else:
            parts = call(
                functools.partial(chosen_kernel, places, last),
                shapes,
                [VMEM] * (len(theirs) + 2),
                [weights],
                micros=2.0,
            )(pick.reshape(1, -1), *theirs, lhs)
        return parts[-1], started(mode, steps, outs, parts)

    if blocks == 8:
        passed = call(
            functools.partial(passed_kernel, last),
            jax.ShapeDtypeStruct(white.shape, bf16),
            [VMEM] * 3,
            micros=0.5,
        )(pair_masks.reshape(1, -1), white, near)
        along_x = apart(passed, "chan", 2)
        along_y = apart(passed, "chan", 4)
    far_done, far_sum = day_sum(FAR, far)
    if days == 4:
        if FAR_FIRST:
            white2, _ = lax.optimization_barrier((white2, far_done))
        near2 = apart(white2, "chan", 1)
        near_kept, near_done = call(
            paired_kernel,
            [jax.ShapeDtypeStruct((slot_rows, 256), f32), jax.ShapeDtypeStruct((slot_rows, 256), bf16)],
            [VMEM] * 4,
            [weights, pltpu.VMEM((2 * slot_rows, 256), f32)],
            micros=2.0,
        )(near, lhs, near2, prepare(white2, 2))
        near_came = [near_kept, apart(near_done, "day", 2)]
    else:
        near_done, near_sum = day_sum("low", near)
        near_came = near_sum()
    if blocks == 8:
        corner = apart(far, "chan", 1)
        if NEAR_FIRST:
            along_x, along_y, _ = lax.optimization_barrier((along_x, along_y, near_done))
        free_done, free_sum = day_sum(FREE, (along_x, along_y, corner), pair_masks)
    else:
        free = white
        third = pair_masks[0] ^ pair_masks[1] ^ pair_masks[2] ^ 1 ^ last
        for bit in range(blocks.bit_length() - 1):
            free = jnp.where(((third >> bit) & 1) == 1, apart(free, "chan", 2**bit), free)
        free_done, free_sum = day_sum(FREE, free)
    far_came = far_sum(free_done if FAR_AFTER else None)
    sums = [near_came, far_came, free_sum((None, near_came[-1], (near_came[-1], far_came[-1]))[LAST_AFTER])]

    day_total = records.shape[0] * days
    norm = float((day_total * window_offsets.shape[1] * L) ** -0.5)

    def finish(names, groups, before=None):
        flat = [part for group in groups for part in group]
        extra = [] if before is None else [before]
        return pl.pallas_call(
            functools.partial(finish_kernel, share, norm, last, names, [len(group) for group in groups]),
            out_shape=jax.ShapeDtypeStruct((3, LAGS, share * chans), f32),
            in_specs=[HBM] + [VMEM] * len(flat) + [HBM] * len(extra),
            out_specs=HBM,
            scratch_shapes=[
                pltpu.VMEM((2, slot_rows, 128), f32),
                pltpu.VMEM((len(names), LAGS, share * chans), f32),
                pltpu.SMEM(pair_masks.shape, jnp.int32),
                pltpu.SemaphoreType.DMA((len(names) + 1,)),
            ],
            input_output_aliases={1 + len(flat): 0} if extra else {},
            compiler_params=pltpu.CompilerParams(vmem_limit_bytes=24 * 1024 * 1024),
            cost_estimate=pl.CostEstimate(flops=int(1e9), bytes_accessed=int(3e6), transcendentals=0),
        )(pair_masks, *flat, *extra)

    return finish(["third"], sums[2:], finish(["near", "far"], sums[:2]))


def solution(mesh):
    in_specs = (P("day", "chan", None), P(), P("day", None), P())
    out_specs = P(None, None, ("chan", "day"))
    return jax.shard_map(local, mesh=mesh, in_specs=in_specs, out_specs=out_specs, check_vma=False)
```

```python
import functools

import jax
import jax.numpy as jnp
from jax import lax
from jax.experimental import pallas as pl
from jax.experimental.pallas import tpu as pltpu
from jax.sharding import PartitionSpec as P

L = 1024
MAXLAG = 32
LAGS = 2 * MAXLAG + 1
FINE = 16
COARSE = 4
PLANES = FINE + 1
PAD = 1152
CUT = 1280
COST = 2.5
DIRECT_ORDER = (2, 3, 1)
FAR_AFTER = False
LAST_AFTER = 1
LATE_Z = False
FAR_FIRST = True
EARLY = False
NEAR_FIRST = False
FAR, FREE = "low", "low"
NT = (((1,), (1,)), ((), ()))
VMEM = pl.BlockSpec(memory_space=pltpu.VMEM)
SMEM = pl.BlockSpec(memory_space=pltpu.SMEM)
HBM = pl.BlockSpec(memory_space=pltpu.HBM)


def call(kernel, out_shape, in_specs, scratch=(), micros=1.0, vmem=24):
    many = isinstance(out_shape, list)
    return pl.pallas_call(
        kernel,
        out_shape=out_shape,
        in_specs=in_specs,
        out_specs=[VMEM] * len(out_shape) if many else VMEM,
        scratch_shapes=list(scratch),
        compiler_params=pltpu.CompilerParams(vmem_limit_bytes=vmem * 1024 * 1024),
        cost_estimate=pl.CostEstimate(flops=int(micros * COST * 1e9), bytes_accessed=int(micros * COST * 3e6), transcendentals=0),
    )


def whiten_kernel(off_hbm, taps_hbm, rec_hbm, out_ref, off_ref, taps_ref, rec_ref, wide_ref, sems):
    copies = [
        pltpu.make_async_copy(src, dst, sems.at[k])
        for k, (src, dst) in enumerate(((off_hbm, off_ref), (rec_hbm, rec_ref), (taps_hbm, taps_ref)))
    ]
    for copy in copies:
        copy.start()
    chans, rec_len = rec_ref.shape[1], rec_ref.shape[2]
    wide_ref[...] = jnp.zeros_like(wide_ref)
    copies[2].wait()
    copies[0].wait()
    taps = taps_ref[...].astype(jnp.float32)
    row = jnp.concatenate([taps, jnp.zeros((1, 384 - taps.shape[1]), jnp.float32)], axis=1)
    row = jnp.broadcast_to(row, (8, 384))
    bands, bases = [], []
    for w in range(2):
        start = off_ref[0, w]
        base = jnp.minimum((start // 128) * 128, rec_len - CUT)
        bases.append(pl.multiple_of(base, 128))
        moved = pltpu.roll(row, start - base, 1)
        block = jnp.broadcast_to(moved[0:1], (128, 384))
        block = pltpu.roll(block, 0, 1, stride=1, stride_axis=0).astype(jnp.bfloat16)
        none = jnp.zeros((128, 128), jnp.bfloat16)
        bands.append(
            jnp.concatenate(
                [jnp.concatenate([block, none], axis=1), jnp.concatenate([none, block], axis=1)],
                axis=0,
            )
        )
    copies[1].wait()
    for w in range(2):
        wide_ref[w, w * chans : (w + 1) * chans, :] = rec_ref[0, :, pl.ds(bases[w], CUT)]
    parts = []
    for c in range(0, L, 512):
        pair = 0.0
        for w in range(2):
            both = jnp.concatenate([wide_ref[w, :, c : c + 512], wide_ref[w, :, c + 256 : c + 768]], axis=0)
            pair += lax.dot_general(bands[w], both, NT, preferred_element_type=jnp.float32)
        parts += [pair[:, 0:128], pair[:, 128:256]]
    power = sum(jnp.sum(part * part, axis=0, keepdims=True) for part in parts) * (1.0 / L)
    scale = lax.rsqrt(power + 1e-06)
    for c, part in enumerate(parts):
        out_ref[c * 256 : (c + 1) * 256, :] = (part * scale).astype(jnp.bfloat16)


def prepare_kernel(days, count, white_ref, lhs_ref):
    chans = white_ref.shape[1] // 2
    share = chans // days
    bits = days.bit_length() - 1
    me = lax.axis_index("day")
    rows = lax.broadcasted_iota(jnp.int32, (2 * chans, 2 * chans), 0)
    cols = lax.broadcasted_iota(jnp.int32, (2 * chans, 2 * chans), 1)
    place = (rows % chans) // share
    slot = jnp.zeros_like(place)
    for b in range(bits):
        slot = slot + (((place >> b) & 1) << (bits - 1 - b))
    source = (rows // chans) * chans + (slot ^ me) * share + rows % share
    pick = (cols == source).astype(jnp.float32).astype(jnp.bfloat16)
    mine = lax.dot_general(pick, white_ref[...], NT, preferred_element_type=jnp.float32)
    mine = jnp.concatenate([mine, jnp.zeros((2 * chans, PAD - L), jnp.float32)], axis=1)
    for p in range(PLANES):
        moved = (pltpu.roll(mine, p, 1) if p else mine).astype(jnp.bfloat16)
        for w in range(2):
            for b in range(count):
                at = (b * PLANES + p) * share
                lhs_ref[at : at + share, w * PAD : (w + 1) * PAD] = moved[w * chans + b * share : w * chans + (b + 1) * share]


def fill_weights(theirs, w_ref):
    theirs = theirs.astype(jnp.float32)
    swapped = pltpu.roll(theirs, 64, 1)
    low = lax.broadcasted_iota(jnp.int32, (1, 128), 1) < 64
    zero = jnp.zeros((16, 128), jnp.float32)
    for w, (a, b) in enumerate(((theirs, swapped), (swapped, theirs))):
        first = jnp.concatenate([zero, zero, a, zero, zero, zero, zero], axis=0)
        second = jnp.concatenate([zero, b, zero, zero, zero, zero, zero], axis=0)
        both = jnp.where(low, first, second).astype(jnp.bfloat16)
        rows = both.shape[0]
        w_ref[w * PAD : w * PAD + rows, 0:128] = both
        w_ref[w * PAD + rows : (w + 1) * PAD, 0:128] = jnp.zeros((PAD - rows, 128), jnp.bfloat16)
        w_ref[w * PAD : w * PAD + rows - 32, 128:256] = both[32:]
        w_ref[w * PAD + rows - 32 : (w + 1) * PAD, 128:256] = jnp.zeros((PAD - rows + 32, 128), jnp.bfloat16)


def correlate(places, theirs, lhs_ref, out_refs, w_ref):
    fill_weights(theirs, w_ref)
    weights = w_ref[...]
    half = lhs_ref.shape[0] // 2
    size = lhs_ref.shape[0] // len(places)
    for base in (half, 0):
        part = jnp.dot(lhs_ref[base : base + half, :], weights, preferred_element_type=jnp.float32)
        for place, (index, at) in enumerate(places):
            row = place * size - base
            if 0 <= row < half:
                ref = out_refs[index]
                ref[at * size : (at + 1) * size, :] = part[row : row + size].astype(ref.dtype)


def paired_kernel(theirs_ref, lhs_ref, theirs2_ref, lhs2_ref, kept_ref, sent_ref, w_ref, sum_ref):
    half = lhs2_ref.shape[0]
    fill_weights(theirs_ref[...], w_ref)
    sum_ref[...] = jnp.dot(lhs_ref[0:half, :], w_ref[...], preferred_element_type=jnp.float32)
    fill_weights(theirs2_ref[...], w_ref)
    total = sum_ref[...] + jnp.dot(lhs2_ref[...], w_ref[...], preferred_element_type=jnp.float32)
    size = kept_ref.shape[0]
    kept_ref[...] = total[0:size]
    sent_ref[...] = total[size:].astype(jnp.bfloat16)


def known_kernel(places, theirs_ref, lhs_ref, *refs):
    correlate(places, theirs_ref[...], lhs_ref, refs[:-1], refs[-1])


def third_mask(masks_ref, last):
    return masks_ref[0] ^ masks_ref[1] ^ masks_ref[2] ^ 1 ^ last


def other_core(third):
    return (third == 3) | (third == 5)


def passed_kernel(last, masks_ref, white_ref, near_ref, out_ref):
    masks = masks_ref[...]
    third = masks[:, 0:1] ^ masks[:, 1:2] ^ masks[:, 2:3] ^ 1 ^ last
    white, near = white_ref[...].astype(jnp.float32), near_ref[...].astype(jnp.float32)
    out_ref[...] = jnp.where(other_core(third), near, white).astype(jnp.bfloat16)


def chosen_kernel(places, last, masks_ref, x_ref, y_ref, corner_ref, lhs_ref, *refs):
    outs, w_ref = refs[:-1], refs[-1]
    masks = masks_ref[...]
    chip = (masks[:, 0:1] ^ masks[:, 1:2] ^ masks[:, 2:3] ^ 1 ^ last) >> 1
    x, y, corner = (ref[...].astype(jnp.float32) for ref in (x_ref, y_ref, corner_ref))
    theirs = jnp.where(chip == 1, x, jnp.where(chip == 2, y, corner))
    correlate(places, theirs, lhs_ref, outs, w_ref)


def finish_kernel(share, norm, last, names, counts, masks_hbm, *refs):
    ins, out_ref, s_ref, plane_ref, masks_ref, sems = list(refs[: sum(counts)]), *refs[-5:]
    fetch = pltpu.make_async_copy(masks_hbm, masks_ref, sems.at[len(names)])
    fetch.start()
    low = lax.broadcasted_iota(jnp.int32, (1, 128), 1) < 64
    rows = PLANES * share
    copies = []
    for k, name in enumerate(names):
        total = sum(ins.pop(0)[0:rows, :].astype(jnp.float32) for _ in range(counts[k])) * norm
        s_ref[0] = total[:, 0:128]
        s_ref[1] = total[:, 128:256]
        for pair in range(share // 2):
            to = slice(pair * 128, pair * 128 + 128)
            for tile in range(COARSE // 2):
                one = s_ref[tile, pl.ds(2 * pair, FINE, stride=share), :]
                two = s_ref[tile, pl.ds(2 * pair + 1, FINE, stride=share), :]
                q = 2 * tile * FINE
                plane_ref[k, q : q + FINE, to] = jnp.where(low, one, pltpu.roll(two, 64, 1))
                plane_ref[k, q + FINE : q + 2 * FINE, to] = jnp.where(low, pltpu.roll(one, 64, 1), two)
            one = s_ref[1, FINE * share + 2 * pair : FINE * share + 2 * pair + 1, :]
            two = s_ref[1, FINE * share + 2 * pair + 1 : FINE * share + 2 * pair + 2, :]
            plane_ref[k, LAGS - 1 : LAGS, to] = jnp.where(low, pltpu.roll(one, 64, 1), two)
        if k == 0:
            fetch.wait()
        mask = {"near": 1, "far": last, "third": third_mask(masks_ref, last)}[name]
        r = jnp.where(masks_ref[0] == mask, 0, jnp.where(masks_ref[1] == mask, 1, 2))
        copies.append(pltpu.make_async_copy(plane_ref.at[k], out_ref.at[r], sems.at[k]))
        copies[-1].start()
    for copy in copies:
        copy.wait()


def apart(value, axis, mask):
    return lax.ppermute(value, axis, [(s, s ^ mask) for s in range(lax.axis_size(axis))])


def local(records, filter_taps, window_offsets, pair_masks):
    chans, rec_len = records.shape[1], records.shape[2]
    taps = filter_taps.shape[0]
    blocks = lax.axis_size("chan")
    days = lax.axis_size("day")
    share = chans // days
    last = blocks - 1
    bf16, f32 = jnp.bfloat16, jnp.float32
    white = call(
        whiten_kernel,
        jax.ShapeDtypeStruct((L, 2 * chans), bf16),
        [HBM] * 3,
        [
            pltpu.SMEM((1, 2), jnp.int32),
            pltpu.VMEM((1, taps), bf16),
            pltpu.VMEM((1, chans, rec_len), bf16),
            pltpu.VMEM((2, 2 * chans, CUT), bf16),
            pltpu.SemaphoreType.DMA((3,)),
        ],
        micros=2.0,
        vmem=63,
    )(window_offsets, filter_taps.reshape(1, -1), records)

    near = apart(white, "chan", 1)
    far = apart(white, "chan", last)
    if days == 4:
        white2 = apart(lax.optimization_barrier((white, near))[0] if LATE_Z else white, "day", 1)

    def prepare(block, count):
        return call(
            functools.partial(prepare_kernel, days, count),
            jax.ShapeDtypeStruct((PLANES * share * count, 2 * PAD), bf16),
            [VMEM],
            micros=1.5,
        )(block)

    lhs = prepare(lax.optimization_barrier((white, near))[0] if EARLY else white, days)

    slot_rows = PLANES * share
    weights = pltpu.VMEM((2 * PAD, 256), bf16)

    def reverse(slot):
        return sum(((slot >> b) & 1) << (days.bit_length() - 2 - b) for b in range(days.bit_length() - 1))

    def plan(mode):
        if mode == "direct":
            return list(DIRECT_ORDER), [([slot], bf16 if slot else f32) for slot in range(days)]
        steps = [1 << b for b in range(days.bit_length() - 1)]
        if mode == "high":
            steps = steps[::-1]
        left, outs = list(range(days)), []
        for step in steps:
            outs.insert(0, ([slot for slot in left if slot & step], bf16 if len(left) == days else f32))
            left = [slot for slot in left if not slot & step]
        return steps, [(left, f32)] + outs

    def started(mode, steps, outs, parts):
        if mode == "direct":
            came = [parts[0]] + [apart(parts[s], "day", s) for s in steps]
            return lambda after=None: came
        kept = list(parts[:-1])
        came = [apart(parts[-1], "day", steps[0])]
        held = [[slot ^ steps[0] for slot in outs[-1][0]]]

        def rest(after=None):
            if after is not None:
                came[0], _ = lax.optimization_barrier((came[0], after))
            for step in steps[1:]:
                piece, slots = kept.pop(), outs[len(kept)][0]
                n = piece.shape[0]
                for c, slots_c in zip(came, held):
                    at = slots_c.index(slots[0]) * slot_rows
                    piece = piece + c[at : at + n].astype(f32)
                held.append([slot ^ step for slot in slots])
                came.append(apart(piece.astype(bf16), "day", step))
            return [kept[0]] + came

        rest.came = came
        return rest

    def day_sum(mode, theirs, pick=None):
        mode = mode if days == 4 else "low"
        steps, outs = plan(mode)
        shapes = [jax.ShapeDtypeStruct((len(slots) * slot_rows, 256), kind) for slots, kind in outs]
        where = {slot: (k, at) for k, (slots, _) in enumerate(outs) for at, slot in enumerate(slots)}
        places = [where[reverse(place)] for place in range(days)]
        if pick is None:
            parts = call(functools.partial(known_kernel, places), shapes, [VMEM] * 2, [weights], micros=2.0)(theirs, lhs)
        else:
            parts = call(
                functools.partial(chosen_kernel, places, last),
                shapes,
                [VMEM] * (len(theirs) + 2),
                [weights],
                micros=2.0,
            )(pick.reshape(1, -1), *theirs, lhs)
        return parts[-1], started(mode, steps, outs, parts)

    if blocks == 8:
        passed = call(
            functools.partial(passed_kernel, last),
            jax.ShapeDtypeStruct(white.shape, bf16),
            [VMEM] * 3,
            micros=0.5,
        )(pair_masks.reshape(1, -1), white, near)
        along_x = apart(passed, "chan", 2)
        along_y = apart(passed, "chan", 4)
    far_done, far_sum = day_sum(FAR, far)
    if days == 4:
        if FAR_FIRST:
            white2, _ = lax.optimization_barrier((white2, far_done))
        near2 = apart(white2, "chan", 1)
        near_kept, near_done = call(
            paired_kernel,
            [jax.ShapeDtypeStruct((slot_rows, 256), f32), jax.ShapeDtypeStruct((slot_rows, 256), bf16)],
            [VMEM] * 4,
            [weights, pltpu.VMEM((2 * slot_rows, 256), f32)],
            micros=2.0,
        )(near, lhs, near2, prepare(white2, 2))
        near_came = [near_kept, apart(near_done, "day", 2)]
    else:
        near_done, near_sum = day_sum("low", near)
        near_came = near_sum()
    if blocks == 8:
        corner = apart(far, "chan", 1)
        if NEAR_FIRST:
            along_x, along_y, _ = lax.optimization_barrier((along_x, along_y, near_done))
        free_done, free_sum = day_sum(FREE, (along_x, along_y, corner), pair_masks)
    else:
        free = white
        third = pair_masks[0] ^ pair_masks[1] ^ pair_masks[2] ^ 1 ^ last
        for bit in range(blocks.bit_length() - 1):
            free = jnp.where(((third >> bit) & 1) == 1, apart(free, "chan", 2**bit), free)
        free_done, free_sum = day_sum(FREE, free)
    far_came = far_sum(free_done if FAR_AFTER else None)
    sums = [near_came, far_came, free_sum((None, near_came[-1], (near_came[-1], far_came[-1]))[LAST_AFTER])]

    day_total = records.shape[0] * days
    norm = float((day_total * window_offsets.shape[1] * L) ** -0.5)

    def finish(names, groups, before=None):
        flat = [part for group in groups for part in group]
        extra = [] if before is None else [before]
        return pl.pallas_call(
            functools.partial(finish_kernel, share, norm, last, names, [len(group) for group in groups]),
            out_shape=jax.ShapeDtypeStruct((3, LAGS, share * chans), f32),
            in_specs=[HBM] + [VMEM] * len(flat) + [HBM] * len(extra),
            out_specs=HBM,
            scratch_shapes=[
                pltpu.VMEM((2, slot_rows, 128), f32),
                pltpu.VMEM((len(names), LAGS, share * chans), f32),
                pltpu.SMEM(pair_masks.shape, jnp.int32),
                pltpu.SemaphoreType.DMA((len(names) + 1,)),
            ],
            input_output_aliases={1 + len(flat): 0} if extra else {},
            compiler_params=pltpu.CompilerParams(vmem_limit_bytes=24 * 1024 * 1024),
            cost_estimate=pl.CostEstimate(flops=int(1e9), bytes_accessed=int(3e6), transcendentals=0),
        )(pair_masks, *flat, *extra)

    return finish(["third"], sums[2:], finish(["near", "far"], sums[:2]))


def solution(mesh):
    in_specs = (P("day", "chan", None), P(), P("day", None), P())
    out_specs = P(None, None, ("chan", "day"))
    return jax.shard_map(local, mesh=mesh, in_specs=in_specs, out_specs=out_specs, check_vma=False)
```
